256 devices in a mesh: expert: 8 (over x, core), fsdp: 32 (over z, y).
Axes of the slice: x: 4, y: 4, z: 8, core: 2. Of those that a mesh axis runs over, the one named last changes fastest.
Arguments:
- weights: bfloat16 [8, 8192, 4608], P('expert', 'fsdp'), may hold values from -0.09375 to 0.09375
- gaussian: bfloat16 [8192, 640], P('fsdp'), may hold values from -6 to 6
Outputs:
- orthonormal: float32 [8, 4608, 640], P('expert', 'fsdp')
- projection: float32 [8, 8192, 640], P('expert', 'fsdp')
The draws below stay inside these ranges and needn't reach their ends.
All inputs are finite; a program needn't handle non-finite values.
Results may differ from the reference program's by a relative error of at most 0.015.
Values may be sent and summed in bfloat16 or wider, within the bound.
A program may use at most 128 MiB of HBM per device.

```python
import jax
import jax.numpy as jnp
from jax import lax

D = 4608
F = 8192
K = 640
E = 8


def levels(stream_key, dims, split, low, high):
    loudness = 1.0
    for dim, blocks in split:
        draws = jax.random.uniform(jax.random.fold_in(jax.random.fold_in(stream_key, 6), dim), (blocks,), jnp.float32, low / len(split), high / len(split))
        loudness = loudness * jnp.repeat(jnp.exp(draws), dims[dim] // blocks).reshape((-1,) + (1,) * (len(dims) - 1 - dim))
    return loudness


def centred(rng, shape, width, most, cuts=(), dtype=jnp.bfloat16):
    entries = width * jax.random.normal(rng, shape, jnp.float32)
    if cuts:
        entries = entries * levels(rng, shape, cuts, -0.22, 0.18)
    return jnp.clip(entries, -most, most).astype(dtype)


def setup_inputs(seed: int = 0) -> dict:
    key_list = jax.random.split(jax.random.key(seed), 3)
    return {
        "weights": centred(key_list[0], (E, F, D), D ** -0.5, 0.09375, ((0, 8), (1, 32))),
        "gaussian": centred(key_list[1], (F, K), 1.0, 6.0, ((0, 32),)),
    }


def reference(weights, gaussian):

    def accumulate(running, member):
        return (running + member.astype(jnp.float32), None)
    summed, unused = lax.scan(accumulate, jnp.zeros((F, D), jnp.float32), weights)
    mean_weight = summed / E

    def compress(member):
        deltas = (member.astype(jnp.float32) - mean_weight).astype(jnp.bfloat16)
        sketch = lax.dot_general(deltas.astype(jnp.float32), gaussian.astype(jnp.float32), (((0,), (0,)), ((), ())), preferred_element_type=jnp.float32)
        gram_matrix = jnp.dot(sketch.T, sketch, precision=lax.Precision.HIGHEST) / D
        lower_factor = jnp.linalg.cholesky(gram_matrix)
        orthonormal = jax.scipy.linalg.solve_triangular(lower_factor, sketch.T, lower=True).T
        projection = jnp.dot(deltas.astype(jnp.float32), orthonormal.astype(jnp.bfloat16).astype(jnp.float32), preferred_element_type=jnp.float32)
        return (orthonormal, projection)
    results = lax.map(compress, weights)
    return (results[0], results[1])
```

```python
import functools
import jax
import jax.numpy as jnp
from jax import lax
from jax.sharding import PartitionSpec as P
from jax.experimental import pallas as pl
from jax.experimental.pallas import tpu as pltpu

MESH = pl.DeviceIdType.MESH
NY, NZ = 4, 8
NB = 128

def rc(src, dst, ss, rs, dev):
    return pltpu.make_async_remote_copy(src_ref=src, dst_ref=dst, send_sem=ss, recv_sem=rs, device_id=dev,
                                        device_id_type=MESH)

def sketch_body(w_ref, g_ref, s_ref, wz_ref, wv, gv, p_ref, sbuf, rbuf, ysend, yrecv, gsend, grecv, fsend, frecv,
           zsend, zrecv, loc, *, SUBS):
    rows, D = w_ref.shape
    K = g_ref.shape[1]
    cw = D // NY
    ch = cw // NZ
    e = lax.axis_index("expert")
    f = lax.axis_index("fsdp")
    y = lax.rem(f, NY)
    z = f // NY
    core = lax.rem(e, 2)
    sib = (e + 1 - 2 * core, f)
    ydev = lambda d: (e, z * NY + lax.rem(y + d, NY))
    zdev = lambda d: (e, lax.rem(z + d + NZ, NZ) * NY + y)
    barrier = pltpu.get_barrier_semaphore()
    partners = [ydev(1), ydev(2), ydev(3), sib, zdev(1), zdev(-1)]
    for p in partners:
        pl.semaphore_signal(barrier, inc=1, device_id=p, device_id_type=MESH)
    pl.semaphore_wait(barrier, len(partners))

    hr = rows // 2
    myrow = pl.multiple_of(y * rows, rows)
    ghalf = pl.multiple_of(core * hr, hr)
    gcs = []
    for d in (1, 3, 2):
        c = rc(g_ref.at[pl.ds(ghalf, hr), :], gv.at[pl.ds(pl.multiple_of(y * rows + ghalf, hr), hr), :],
               gsend.at[d], grecv.at[d], ydev(d))
        c.start(); gcs.append((d, c))
    wcs = []
    for d in (1, 3, 2):
        yy = lax.rem(y + d, NY)
        c = rc(w_ref.at[:, pl.ds(pl.multiple_of(yy * cw, NB), cw)], wv.at[pl.ds(myrow, rows), :],
               ysend.at[d], yrecv.at[d], ydev(d))
        c.start(); wcs.append((d, c))
    lw = pltpu.make_async_copy(w_ref.at[:, pl.ds(pl.multiple_of(y * cw, NB), cw)], wv.at[pl.ds(myrow, rows), :], loc.at[0])
    lw.start()
    lg = pltpu.make_async_copy(g_ref, gv.at[pl.ds(myrow, rows), :], loc.at[1])
    lg.start()
    fcs = []
    for d, c in gcs:
        c.wait_recv()
        src = lax.rem(y - d + NY, NY)
        piece = pl.ds(pl.multiple_of(src * rows + ghalf, hr), hr)
        h = rc(gv.at[piece, :], gv.at[piece, :], fsend.at[d], frecv.at[d], sib)
        h.start(); fcs.append(h)
    lw.wait(); lg.wait()
    for h in fcs:
        h.wait_recv()
    for d, c in wcs:
        c.wait_recv()
    out = pltpu.make_async_copy(wv, wz_ref, loc.at[2])
    out.start()

    def block(i, _):
        o = pl.multiple_of(i * NB, NB)
        p_ref[pl.ds(o, NB), :] = lax.dot_general(wv[:, pl.ds(o, NB)], gv[...], (((0,), (0,)), ((), ())),
                                                 preferred_element_type=jnp.float32)
        return 0
    lax.fori_loop(0, cw // NB, block, 0)

    ha = 80
    prev = {}
    def own(t, r, n, c0, c1):
        return p_ref[pl.ds(pl.multiple_of(t * ch + r, 16), n), c0:c1]
    for s in range(4):
        for dr, sgn in ((0, 1), (1, -1)):
            t = lax.rem(z + sgn * (4 - s) + NZ, NZ)
            for u, (c0, c1) in enumerate(SUBS):
                if s == 0:
                    r, n = (0, ha) if dr == 0 else (ha, ch - ha)
                    sbuf[dr, s, r:r + n, c0:c1] = own(t, r, n, c0, c1).astype(jnp.bfloat16)
                else:
                    prev[dr, u].wait_recv()
                    if s == 1:
                        r, n = (0, ha) if dr == 0 else (ha, ch - ha)
                        q, m = (ha, ch - ha) if dr == 0 else (0, ha)
                        sbuf[dr, s, r:r + n, c0:c1] = (own(t, r, n, c0, c1) + rbuf[dr, 0, r:r + n, c0:c1].astype(jnp.float32)).astype(jnp.bfloat16)
                        sbuf[dr, s, q:q + m, c0:c1] = own(t, q, m, c0, c1).astype(jnp.bfloat16)
                    else:
                        sbuf[dr, s, :, c0:c1] = (own(t, 0, ch, c0, c1) + rbuf[dr, s - 1, :, c0:c1].astype(jnp.float32)).astype(jnp.bfloat16)
                    prev[dr, u].wait_send()
                    r, n = 0, ch
                c = rc(sbuf.at[dr, s, pl.ds(r, n), pl.ds(c0, c1 - c0)], rbuf.at[dr, s, pl.ds(r, n), pl.ds(c0, c1 - c0)],
                       zsend.at[dr, s, u], zrecv.at[dr, s, u], zdev(sgn))
                c.start()
                prev[dr, u] = c
    for u, (c0, c1) in enumerate(SUBS):
        prev[0, u].wait()
        prev[1, u].wait()
        s_ref[:, c0:c1] = (own(z, 0, ch, c0, c1) + rbuf[0, 3, :, c0:c1].astype(jnp.float32)
                           + rbuf[1, 3, :, c0:c1].astype(jnp.float32))
    for d, c in gcs:
        c.wait_send()
    for d, c in wcs:
        c.wait_send()
    for h in fcs:
        h.wait_send()
    out.wait()

def sketch_kernel(w, g, subs=((0, 384), (384, 640))):
    rows, D = w.shape; K = g.shape[1]
    cw = D // NY; ch = cw // NZ
    nu = len(subs)
    V = pl.BlockSpec(memory_space=pltpu.VMEM); A = pl.BlockSpec(memory_space=pl.ANY)
    DM = pltpu.SemaphoreType.DMA
    return pl.pallas_call(
        functools.partial(sketch_body, SUBS=subs),
        out_shape=(jax.ShapeDtypeStruct((ch, K), jnp.float32), jax.ShapeDtypeStruct((rows * NY, cw), jnp.bfloat16)),
        in_specs=[A, A], out_specs=(V, A),
        scratch_shapes=[pltpu.VMEM((rows * NY, cw), jnp.bfloat16), pltpu.VMEM((rows * NY, K), jnp.bfloat16),
                        pltpu.VMEM((cw, K), jnp.float32),
                        pltpu.VMEM((2, 4, ch, K), jnp.bfloat16), pltpu.VMEM((2, 4, ch, K), jnp.bfloat16),
                        DM((4,)), DM((4,)), DM((4,)), DM((4,)), DM((4,)), DM((4,)),
                        DM((2, 4, nu)), DM((2, 4, nu)), DM((3,))],
        compiler_params=pltpu.CompilerParams(collective_id=0, has_side_effects=True, vmem_limit_bytes=48 * 2**20),
        name="sketch_exchange",
    )(w, g)


HI = lax.Precision.HIGHEST


def base_inverse(t_ref, n_ref):
    sub = lax.broadcasted_iota(jnp.int32, (8, NB), 0)
    row = lax.broadcasted_iota(jnp.int32, (NB, NB), 0)
    col = lax.broadcasted_iota(jnp.int32, (NB, NB), 1)
    n_ref[...] = jnp.where(row == col, 1.0, 0.0).astype(jnp.float32)
    nsub = NB // 8
    cur_t, cur_n = t_ref[0:8, :], n_ref[0:8, :]
    for b in range(nsub):
        r0 = 8 * b
        last = b == nsub - 1
        c = [jnp.broadcast_to(cur_t[:, r0 + i:r0 + i + 1], (8, NB)) for i in range(8)]
        if not last:
            nt, nn = t_ref[r0 + 8:r0 + 16, :], n_ref[r0 + 8:r0 + 16, :]
            d = [jnp.broadcast_to(nt[:, r0 + i:r0 + i + 1], (8, NB)) for i in range(8)]
        for i in range(8):
            rs = lax.rsqrt(jnp.broadcast_to(c[i][i:i + 1, :], (8, NB)))
            m = c[i] * rs
            mk = {}
            for k in range(i + 1, 8):
                mk[k] = jnp.broadcast_to(m[k:k + 1, :], (8, NB))
                c[k] = c[k] - m * mk[k]
            mm = jnp.where(sub > i, m, 0.0)
            ft = jnp.broadcast_to(cur_t[i:i + 1, :], (8, NB)) * rs
            fn = jnp.broadcast_to(cur_n[i:i + 1, :], (8, NB)) * rs
            cur_t = jnp.where(sub == i, ft, cur_t - mm * ft)
            cur_n = jnp.where(sub == i, fn, cur_n - mm * fn)
            if not last:
                md = d[i] * rs
                for k in range(i + 1, 8):
                    d[k] = d[k] - md * mk[k]
                nt = nt - md * ft
                nn = nn - md * fn
        n_ref[r0:r0 + 8, :] = cur_n
        if not last:
            if b < nsub - 2:
                lt = cur_t[:, :]
                both = jnp.concatenate([cur_t, cur_n], axis=1)
                upd = lax.dot_general(lt, both, (((0,), (0,)), ((), ())), precision=HI,
                                      preferred_element_type=jnp.float32)
                t_ref[r0 + 16:, :] = t_ref[r0 + 16:, :] - upd[r0 + 16:, :NB]
                n_ref[r0 + 16:, :] = n_ref[r0 + 16:, :] - upd[r0 + 16:, NB:]
            cur_t, cur_n = nt, nn

def basis_body(gram_ref, s_ref, o_ref, ob_ref, x_ref, t_ref, n_ref, *, K, D):
    R = s_ref.shape[0]
    x_ref[0:K, :] = gram_ref[...] * (1.0 / D)
    x_ref[K:K + R, :] = s_ref[...]
    def step(j, _):
        off = pl.multiple_of(j * NB, NB)
        t_ref[...] = x_ref[pl.ds(off, NB), pl.ds(off, NB)]
        base_inverse(t_ref, n_ref)
        p = lax.dot_general(x_ref[:, pl.ds(off, NB)], n_ref[...], (((1,), (1,)), ((), ())), precision=HI,
                            preferred_element_type=jnp.float32)
        x_ref[K:K + R, pl.ds(off, NB)] = p[K:K + R]
        r = lax.broadcasted_iota(jnp.int32, (K, NB), 0)
        lk = jnp.where(r >= off + NB, p[0:K], 0.0)
        @pl.when(j < K // NB - 1)
        def _():
            x_ref[...] = x_ref[...] - lax.dot_general(p, lk, (((1,), (1,)), ((), ())), precision=HI,
                                                      preferred_element_type=jnp.float32)
        return 0
    lax.fori_loop(0, K // NB, step, 0)
    o_ref[...] = x_ref[K:K + R, :]
    ob_ref[...] = x_ref[K:K + R, :].astype(jnp.bfloat16)

def chol_basis(gram, s, D):
    K = gram.shape[0]; R = s.shape[0]
    return pl.pallas_call(
        functools.partial(basis_body, K=K, D=D),
        out_shape=(jax.ShapeDtypeStruct((R, K), jnp.float32), jax.ShapeDtypeStruct((R, K), jnp.bfloat16)),
        in_specs=[pl.BlockSpec(memory_space=pltpu.VMEM)] * 2,
        out_specs=(pl.BlockSpec(memory_space=pltpu.VMEM), pl.BlockSpec(memory_space=pltpu.VMEM)),
        scratch_shapes=[pltpu.VMEM((K + R, K), jnp.float32), pltpu.VMEM((NB, NB), jnp.float32),
                        pltpu.VMEM((NB, NB), jnp.float32)],
        compiler_params=pltpu.CompilerParams(vmem_limit_bytes=40 * 2**20),
        name="cholesky_basis",
    )(gram, s)


def project_body(b_ref, wz_ref, m_ref, o_ref, bz, dz, sbuf, rbuf, zsend, zrecv, ysend, yrecv, *, E):
    ch, K = b_ref.shape
    rr, cw = wz_ref.shape
    rows = rr // NY
    e = lax.axis_index("expert")
    f = lax.axis_index("fsdp")
    y = lax.rem(f, NY)
    z = f // NY
    ydev = lambda d: (e, z * NY + lax.rem(y + d + NY, NY))
    zdev = lambda d: (e, lax.rem(z + d + NZ, NZ) * NY + y)
    barrier = pltpu.get_barrier_semaphore()
    partners = [ydev(1), ydev(-1), zdev(1), zdev(-1)]
    for p in partners:
        pl.semaphore_signal(barrier, inc=1, device_id=p, device_id_type=MESH)
    bz[pl.ds(pl.multiple_of(z * ch, 16), ch), :] = b_ref[...]
    pl.semaphore_wait(barrier, len(partners))
    ha = 80
    cs = {}
    def blk(t, r, n):
        return pl.ds(pl.multiple_of(lax.rem(t + NZ, NZ) * ch + r, 16), n)
    def send(dr, s):
        sgn = 1 - 2 * dr
        r, n = (0, ch) if s < 3 else ((0, ha) if dr == 0 else (ha, ch - ha))
        at = bz.at[blk(z - sgn * s, r, n), :]
        c = rc(at, at, zsend.at[dr, s], zrecv.at[dr, s], zdev(sgn))
        c.start()
        cs[dr, s] = c
    send(0, 0); send(1, 0)
    def delta(i, _):
        r = pl.ds(pl.multiple_of(i * 64, 64), 64)
        dz[r, :] = (wz_ref[r, :].astype(jnp.float32) - m_ref[r, :].astype(jnp.float32) * (1.0 / E)).astype(jnp.bfloat16)
        return 0
    lax.fori_loop(0, rr // 64, delta, 0)
    for s in range(1, 4):
        for dr in (0, 1):
            cs[dr, s - 1].wait_recv()
            send(dr, s)
    for dr in (0, 1):
        cs[dr, 3].wait_recv()
    def part(d, r, n):
        yy = lax.rem(y + d + NY, NY)
        return jnp.dot(dz[pl.ds(pl.multiple_of(yy * rows + r, 16), n), :], bz[...], preferred_element_type=jnp.float32)
    h = rows // 2
    ys = {}
    def ysnd(dr, s, r, n):
        c = rc(sbuf.at[dr, s, pl.ds(r, n), :], rbuf.at[dr, s, pl.ds(r, n), :], ysend.at[dr, s], yrecv.at[dr, s],
               ydev(1 - 2 * dr))
        c.start()
        ys[dr, s] = c
    for dr in (0, 1):
        sbuf[dr, 0, h * dr:h * dr + h, :] = part(2, h * dr, h).astype(jnp.bfloat16)
        ysnd(dr, 0, h * dr, h)
    for dr in (0, 1):
        pt = part(1 - 2 * dr, 0, rows)
        a, b = h * dr, h * (1 - dr)
        sbuf[dr, 1, b:b + h, :] = pt[b:b + h].astype(jnp.bfloat16)
        ys[dr, 0].wait_recv()
        sbuf[dr, 1, a:a + h, :] = (pt[a:a + h] + rbuf[dr, 0, a:a + h, :].astype(jnp.float32)).astype(jnp.bfloat16)
        ysnd(dr, 1, 0, rows)
    o_ref[...] = part(0, 0, rows)
    for dr in (0, 1):
        ys[dr, 1].wait_recv()
        o_ref[...] += rbuf[dr, 1].astype(jnp.float32)
    for c in list(cs.values()) + list(ys.values()):
        c.wait_send()

def project_kernel(b, wz, m, E):
    ch, K = b.shape; rr, cw = wz.shape
    rows = rr // NY
    V = pl.BlockSpec(memory_space=pltpu.VMEM)
    DM = pltpu.SemaphoreType.DMA
    return pl.pallas_call(
        functools.partial(project_body, E=E),
        out_shape=jax.ShapeDtypeStruct((rows, K), jnp.float32),
        in_specs=[V, V, V], out_specs=V,
        scratch_shapes=[pltpu.VMEM((ch * NZ, K), jnp.bfloat16), pltpu.VMEM((rr, cw), jnp.bfloat16),
                        pltpu.VMEM((2, 2, rows, K), jnp.bfloat16), pltpu.VMEM((2, 2, rows, K), jnp.bfloat16),
                        DM((2, 4)), DM((2, 4)), DM((2, 2)), DM((2, 2))],
        compiler_params=pltpu.CompilerParams(collective_id=1, has_side_effects=True, vmem_limit_bytes=48 * 2**20),
        name="project_exchange",
    )(b, wz, m)


def on_device(weights, gaussian):
    experts = lax.axis_size("expert")
    d = weights.shape[2]
    own, wz = sketch_kernel(weights[0], gaussian)
    summed = lax.psum(wz, "expert")
    sketch = own - lax.psum(own, "expert") / experts
    gram = lax.psum(jnp.dot(sketch.T, sketch, precision=lax.Precision.HIGHEST), "fsdp")
    orthonormal, basis = chol_basis(gram, sketch, d)
    perm = [(z * NY + y, y * NZ + z) for z in range(NZ) for y in range(NY)]
    placed = lax.ppermute(orthonormal, "fsdp", perm)
    projection = project_kernel(basis, wz, summed, experts)
    return (placed[None], projection[None])


def solution(mesh):
    in_specs = (P("expert", "fsdp", None), P("fsdp", None))
    out_specs = (P("expert", "fsdp", None), P("expert", "fsdp", None))
    return jax.shard_map(
        on_device, mesh=mesh, in_specs=in_specs, out_specs=out_specs, check_vma=False
    )
```

```python
import functools
import jax
import jax.numpy as jnp
from jax import lax
from jax.sharding import PartitionSpec as P
from jax.experimental import pallas as pl
from jax.experimental.pallas import tpu as pltpu

MESH = pl.DeviceIdType.MESH
NX, NY, NZ = 4, 4, 8
NB = 128
F32, BF16 = jnp.float32, jnp.bfloat16


def rc(src, dst, ss, rs, dev):
    return pltpu.make_async_remote_copy(src_ref=src, dst_ref=dst, send_sem=ss, recv_sem=rs, device_id=dev,
                                        device_id_type=MESH)


def place():
    e = lax.axis_index("expert")
    f = lax.axis_index("fsdp")
    x, core, y, z = e // 2, lax.rem(e, 2), lax.rem(f, NY), f // NY
    xdev = lambda d: (lax.rem(x + d + NX, NX) * 2 + core, f)
    ydev = lambda d: (e, z * NY + lax.rem(y + d + NY, NY))
    zdev = lambda d: (e, lax.rem(z + d + NZ, NZ) * NY + y)
    return x, core, y, z, xdev, ydev, zdev, (e + 1 - 2 * core, f)


def greet(partners):
    barrier = pltpu.get_barrier_semaphore()
    for p in partners:
        pl.semaphore_signal(barrier, inc=1, device_id=p, device_id_type=MESH)
    pl.semaphore_wait(barrier, len(partners))


def at(start, size, unit):
    return pl.ds(pl.multiple_of(start, unit), size)


def sketch_body(w_ref, g_ref, s_ref, wz_ref, wv, gv, p_ref, sbuf, rbuf, sp, sx, tb, tr, mo, mr,
           wsend, wrecv, gsend, grecv, fsend, frecv, zsend, zrecv, csend, crecv, xsend, xrecv, hsend, hrecv, loc, *, SUBS):
    rows, D = w_ref.shape
    K = g_ref.shape[1]
    cw = D // NY
    ch = cw // NZ
    ex = ch - NB
    x, core, y, z, xdev, ydev, zdev, sib = place()
    greet([ydev(1), ydev(2), ydev(3), sib, zdev(1), zdev(-1), xdev(1), xdev(2), xdev(3)])

    hr = rows // 2
    mine = at(y * rows, rows, rows)
    gcs = []
    for d in (1, 3, 2):
        c = rc(g_ref.at[at(core * hr, hr, hr), :], gv.at[at(y * rows + core * hr, hr, hr), :],
               gsend.at[d], grecv.at[d], ydev(d))
        c.start()
        gcs.append((d, c))
    lg = pltpu.make_async_copy(g_ref, gv.at[mine, :], loc.at[0])
    lg.start()
    seq = [NZ] + [lax.rem(z + k + 2 * NZ, NZ) for k in (4, 3, 5, 2, 6, 1, 7, 0)]
    wcs = []
    lws = []
    for k, b in enumerate(seq):
        lw = pltpu.make_async_copy(w_ref.at[:, at(y * cw + b * NB, NB, NB)], wv.at[mine, at(b * NB, NB, NB)], loc.at[2 + k])
        lw.start()
        lws.append(lw)
        now = []
        for d in (1, 3, 2):
            yy = lax.rem(y + d, NY)
            c = rc(w_ref.at[:, at(yy * cw + b * NB, NB, NB)], wv.at[mine, at(b * NB, NB, NB)],
                   wsend.at[k, d], wrecv.at[k, d], ydev(d))
            c.start()
            now.append(c)
        wcs.append(now)
    fcs = []
    for d, c in gcs:
        c.wait_recv()
        piece = at(lax.rem(y - d + NY, NY) * rows + core * hr, hr, hr)
        h = rc(gv.at[piece, :], gv.at[piece, :], fsend.at[d], frecv.at[d], sib)
        h.start()
        fcs.append(h)
    lg.wait()
    for h in fcs:
        h.wait_recv()

    def product(k):
        lws[k].wait()
        for c in wcs[k]:
            c.wait_recv()
        o = at(seq[k] * NB, NB, NB)
        p_ref[o, :] = lax.dot_general(wv[:, o], gv[...], (((0,), (0,)), ((), ())), preferred_element_type=F32)

    ha = 64
    prev = {}

    def own(t, r, n, c0, c1):
        if r < NB:
            head = p_ref[at(t * NB + r, min(n, NB - r), 16), c0:c1]
            if r + n <= NB:
                return head
            return jnp.concatenate([head, p_ref[at(NZ * NB + t * ex, ex, 16), c0:c1]], axis=0)

    product(0)
    for s in range(4):
        for k in ((1,), (2, 3), (4, 5), (6, 7))[s]:
            product(k)
        for u, (c0, c1) in enumerate(SUBS):
            for dr, sgn in ((0, 1), (1, -1)):
                t = lax.rem(z + sgn * (4 - s) + NZ, NZ)
                a, m = (0, ha) if dr == 0 else (ha, ch - ha)
                q, l = (ha, ch - ha) if dr == 0 else (0, ha)
                if s:
                    prev[dr, u].wait_recv()
                if s == 0:
                    sbuf[dr, s, a:a + m, c0:c1] = own(t, a, m, c0, c1).astype(BF16)
                    r, n = a, m
                elif s == 1:
                    sbuf[dr, s, a:a + m, c0:c1] = (own(t, a, m, c0, c1) + rbuf[dr, 0, a:a + m, c0:c1].astype(F32)).astype(BF16)
                    sbuf[dr, s, q:q + l, c0:c1] = own(t, q, l, c0, c1).astype(BF16)
                    r, n = 0, ch
                else:
                    sbuf[dr, s, :, c0:c1] = (own(t, 0, ch, c0, c1) + rbuf[dr, s - 1, :, c0:c1].astype(F32)).astype(BF16)
                    r, n = 0, ch
                if s:
                    prev[dr, u].wait_send()
                c = rc(sbuf.at[dr, s, pl.ds(r, n), pl.ds(c0, c1 - c0)], rbuf.at[dr, s, pl.ds(r, n), pl.ds(c0, c1 - c0)],
                       zsend.at[dr, s, u], zrecv.at[dr, s, u], zdev(sgn))
                c.start()
                prev[dr, u] = c
    product(8)
    out = pltpu.make_async_copy(wv, wz_ref, loc.at[1])
    out.start()
    hm = 80
    half = at((ch - hm) * core, hm, 16)
    pairs = []
    for u, (c0, c1) in enumerate(SUBS):
        prev[0, u].wait()
        prev[1, u].wait()
        sp[:, c0:c1] = (own(z, 0, ch, c0, c1) + rbuf[0, 3, :, c0:c1].astype(F32) + rbuf[1, 3, :, c0:c1].astype(F32))
        c = rc(sp.at[:, pl.ds(c0, c1 - c0)], sx.at[:, pl.ds(c0, c1 - c0)], csend.at[u], crecv.at[u], sib)
        c.start()
        pairs.append(c)
    xs = []
    for u, (c0, c1) in enumerate(SUBS):
        pairs[u].wait_recv()
        mo[:, c0:c1] = sp[half, c0:c1] + sx[half, c0:c1]
        tb[:, c0:c1] = mo[:, c0:c1].astype(BF16)
        now = []
        for d in (1, 3, 2):
            c = rc(tb.at[:, pl.ds(c0, c1 - c0)], tr.at[d, :, pl.ds(c0, c1 - c0)], xsend.at[u, d], xrecv.at[u, d], xdev(d))
            c.start()
            now.append(c)
        xs.append(now)
    hs = []
    for u, (c0, c1) in enumerate(SUBS):
        for c in xs[u]:
            c.wait_recv()
        mo[:, c0:c1] = (mo[:, c0:c1] + tr[1, :, c0:c1].astype(F32) + tr[2, :, c0:c1].astype(F32)
                        + tr[3, :, c0:c1].astype(F32)) * (1.0 / (2 * NX))
        h = rc(mo.at[:, pl.ds(c0, c1 - c0)], mr.at[:, pl.ds(c0, c1 - c0)], hsend.at[u], hrecv.at[u], sib)
        h.start()
        hs.append(h)
        s_ref[half, c0:c1] = sp[half, c0:c1] - mo[:, c0:c1]
    rest = at(hm * (1 - core), ch - hm, 16)
    for u, (c0, c1) in enumerate(SUBS):
        hs[u].wait_recv()
        s_ref[rest, c0:c1] = sp[rest, c0:c1] - mr[at((2 * hm - ch) * (1 - core), ch - hm, 16), c0:c1]
    for c in [c for _, c in gcs] + fcs + [c for now in wcs + xs for c in now] + pairs + hs:
        c.wait_send()
    out.wait()


def sketch_kernel(w, g, subs=((0, 384), (384, 640))):
    rows, D = w.shape
    K = g.shape[1]
    cw = D // NY
    ch = cw // NZ
    nu = len(subs)
    V = pl.BlockSpec(memory_space=pltpu.VMEM)
    A = pl.BlockSpec(memory_space=pl.ANY)
    DM = pltpu.SemaphoreType.DMA
    M = pltpu.VMEM
    return pl.pallas_call(
        functools.partial(sketch_body, SUBS=subs),
        out_shape=(jax.ShapeDtypeStruct((ch, K), F32), jax.ShapeDtypeStruct((rows * NY, cw), BF16)),
        in_specs=[A, A], out_specs=(V, A),
        scratch_shapes=[M((rows * NY, cw), BF16), M((rows * NY, K), BF16), M((cw, K), F32),
                        M((2, 4, ch, K), BF16), M((2, 4, ch, K), BF16),
                        M((ch, K), F32), M((ch, K), F32), M((80, K), BF16), M((4, 80, K), BF16), M((80, K), F32), M((80, K), F32),
                        DM((9, 4)), DM((9, 4)), DM((4,)), DM((4,)), DM((4,)), DM((4,)),
                        DM((2, 4, nu)), DM((2, 4, nu)), DM((nu,)), DM((nu,)), DM((nu, 4)), DM((nu, 4)), DM((nu,)), DM((nu,)),
                        DM((11,))],
        compiler_params=pltpu.CompilerParams(collective_id=0, has_side_effects=True, vmem_limit_bytes=48 * 2**20),
        name="sketch_exchange",
    )(w, g)


HI = lax.Precision.HIGHEST
GROUPS = ((0, 768), (768, 1280))
STACK = 2048


def base_inverse(t_ref, n_ref):
    sub = lax.broadcasted_iota(jnp.int32, (8, NB), 0)
    row = lax.broadcasted_iota(jnp.int32, (NB, NB), 0)
    col = lax.broadcasted_iota(jnp.int32, (NB, NB), 1)
    n_ref[...] = jnp.where(row == col, 1.0, 0.0).astype(F32)
    nsub = NB // 8
    wide = lambda v: jnp.broadcast_to(v, (8, NB))
    cur_t, cur_n = t_ref[0:8, :], n_ref[0:8, :]
    for b in range(nsub):
        r0 = 8 * b
        last = b == nsub - 1
        c = [wide(cur_t[:, r0 + i:r0 + i + 1]) for i in range(8)]
        if not last:
            nt, nn = t_ref[r0 + 8:r0 + 16, :], n_ref[r0 + 8:r0 + 16, :]
            d = [wide(nt[:, r0 + i:r0 + i + 1]) for i in range(8)]
        for i in range(8):
            rs = lax.rsqrt(wide(c[i][i:i + 1, :]))
            m = c[i] * rs
            mk = {}
            for k in range(i + 1, 8):
                mk[k] = wide(m[k:k + 1, :])
                c[k] = c[k] - m * mk[k]
            mm = jnp.where(sub > i, m, 0.0)
            ft = wide(cur_t[i:i + 1, :]) * rs
            fn = wide(cur_n[i:i + 1, :]) * rs
            cur_t = jnp.where(sub == i, ft, cur_t - mm * ft)
            cur_n = jnp.where(sub == i, fn, cur_n - mm * fn)
            if not last:
                md = d[i] * rs
                for k in range(i + 1, 8):
                    d[k] = d[k] - md * mk[k]
                nt = nt - md * ft
                nn = nn - md * fn
        n_ref[r0:r0 + 8, :] = cur_n
        if not last:
            if b < nsub - 2:
                both = jnp.concatenate([cur_t, cur_n], axis=1)
                upd = lax.dot_general(cur_t, both, (((0,), (0,)), ((), ())), precision=HI, preferred_element_type=F32)
                t_ref[r0 + 16:, :] = t_ref[r0 + 16:, :] - upd[r0 + 16:, :NB]
                n_ref[r0 + 16:, :] = n_ref[r0 + 16:, :] - upd[r0 + 16:, NB:]
            cur_t, cur_n = nt, nn


def basis_body(s_ref, wz_ref, orth_ref, proj_ref, gp, gr, yr0, yr1, yb0, yb1, zr0, zr1, qf0, qf1,
           fw, fb, fr, mw, dz, x_ref, t_ref, n_ref, bc, bn, ysb, yrb, ob,
           f1s, f1r, f2s, f2r, f3s, f3r, f4s, f4r, ys1, yr1s, zs1, zr1s, zs2, zr2s, ys2, yr2s,
           bs, br, ps, pr, os_, or_):
    ch, K = s_ref.shape
    rr, cw = wz_ref.shape
    rows = rr // NY
    D = cw * NY
    nb = K // NB
    ex = ch - NB
    x, core, y, z, xdev, ydev, zdev, sib = place()
    zd = (1, 7, 2, 6, 3, 5, 4)
    yd = (1, 3, 2)
    greet([ydev(d) for d in yd] + [zdev(d) for d in zd] + [xdev(d) for d in yd] + [sib])

    hf = rr // 2
    f1 = rc(wz_ref.at[at(hf * (1 - core), hf, hf), :], fw, f1s.at[0], f1r.at[0], sib)
    f1.start()
    r0 = 0
    starts = []
    for j in range(nb):
        n = K - j * NB
        gp[r0:r0 + n, :] = lax.dot_general(s_ref[:, j * NB:], s_ref[:, j * NB:(j + 1) * NB], (((0,), (0,)), ((), ())),
                                           precision=HI, preferred_element_type=F32)
        starts.append(r0)
        r0 += n
    gp[r0:, :] = jnp.zeros((STACK - r0, NB), F32)
    done = [f1]
    yrg, ybg, zrg, qfg = (yr0, yr1), (yb0, yb1), (zr0, zr1), (qf0, qf1)
    p1 = []
    for g, (a, n) in enumerate(GROUPS):
        q = n // NY
        now = []
        for d in yd:
            yy = lax.rem(y + d, NY)
            c = rc(gp.at[at(a + q * yy, q, 8), :], yrg[g].at[d], ys1.at[g, d], yr1s.at[g, d], ydev(d))
            c.start()
            now.append(c)
        p1.append(now)
    f1.wait_recv()
    step = 64

    def pair(i, _):
        o = at(i * step, step, step)
        fb[o, :] = (wz_ref[at(hf * core + i * step, step, step), :].astype(F32) + fw[o, :].astype(F32)).astype(BF16)
        return 0
    lax.fori_loop(0, hf // step, pair, 0)
    qx = hf // NX
    f2 = []
    for d in yd:
        xx = lax.rem(x + d, NX)
        c = rc(fb.at[at(qx * xx, qx, qx), :], fr.at[d], f2s.at[d], f2r.at[d], xdev(d))
        c.start()
        f2.append(c)
    p2 = []
    for g, (a, n) in enumerate(GROUPS):
        q = n // NY
        m = q // NZ
        for c in p1[g]:
            c.wait_recv()
        ybg[g][...] = gp[at(a + q * y, q, 8), :] + yrg[g][1] + yrg[g][2] + yrg[g][3]
        now = []
        for d in zd:
            zz = lax.rem(z + d, NZ)
            c = rc(ybg[g].at[at(m * zz, m, 8), :], zrg[g].at[d], zs1.at[g, d], zr1s.at[g, d], zdev(d))
            c.start()
            now.append(c)
        p2.append(now)
    p3 = []
    for g, (a, n) in enumerate(GROUPS):
        m = n // NY // NZ
        for c in p2[g]:
            c.wait_recv()
        here = at(m * z, m, 8)
        tot = ybg[g][here, :]
        for d in range(1, NZ):
            tot = tot + zrg[g][d]
        qfg[g][here, :] = tot * (1.0 / D)
        now = []
        for d in zd:
            c = rc(qfg[g].at[here, :], qfg[g].at[here, :], zs2.at[g, d], zr2s.at[g, d], zdev(d))
            c.start()
            now.append(c)
        p3.append(now)
    for c in f2:
        c.wait_recv()
    mine = at(hf * core + qx * x, qx, qx)

    def four(i, _):
        o = at(i * 32, 32, 32)
        mw[at(hf * core + qx * x + i * 32, 32, 32), :] = (
            fb[at(qx * x + i * 32, 32, 32), :].astype(F32) + fr[1, o, :].astype(F32) + fr[2, o, :].astype(F32)
            + fr[3, o, :].astype(F32)).astype(BF16)
        return 0
    lax.fori_loop(0, qx // 32, four, 0)
    f3 = []
    for d in yd:
        c = rc(mw.at[mine, :], mw.at[mine, :], f3s.at[d], f3r.at[d], xdev(d))
        c.start()
        f3.append(c)
    p4 = []
    for g, (a, n) in enumerate(GROUPS):
        q = n // NY
        for c in p3[g]:
            c.wait_recv()
        here = at(a + q * y, q, 8)
        now = []
        for d in yd:
            c = rc(qfg[g], gr.at[here, :], ys2.at[g, d], yr2s.at[g, d], ydev(d))
            c.start()
            now.append(c)
        gr[here, :] = qfg[g][...]
        p4.append(now)
    for c in f3:
        c.wait_recv()
    f4 = rc(mw.at[at(hf * core, hf, hf), :], mw.at[at(hf * core, hf, hf), :], f4s.at[0], f4r.at[0], sib)
    f4.start()
    f4.wait_recv()

    def delta(i, _):
        o = at(i * step, step, step)
        dz[o, :] = (wz_ref[o, :].astype(F32) - mw[o, :].astype(F32) * (1.0 / (2 * NX))).astype(BF16)
        return 0
    lax.fori_loop(0, rr // step, delta, 0)
    done += f2 + f3 + [f4] + [c for ph in (p1, p2, p3, p4) for now in ph for c in now]

    x_ref[0:K, :] = jnp.zeros((K, K), F32)
    x_ref[K:K + ch, :] = s_ref[...]
    for c in p4[0]:
        c.wait_recv()
    x_ref[0:K, 0:NB] = gr[0:K, :]

    def basis_copy(j, d):
        cols = at(j * NB, NB, NB)
        return rc(bc.at[z, :, cols], bc.at[z, :, cols], bs.at[j, d], br.at[j, d], zdev(d))

    def part_copy(j, d):
        cols = at(j * NB, NB, NB)
        return rc(ysb.at[d, :, cols], yrb.at[d, :, cols], ps.at[j, d], pr.at[j, d], ydev(d))

    ysrc = z // 2

    def orth_copy(j, d):
        cols = at(j * NB, NB, NB)
        t = 4 * lax.rem(z, 2) + lax.rem(y + d, NY)
        return rc(bn.at[at(t * ch, ch, 16), cols], ob.at[:, cols], os_.at[j, d], or_.at[j], ydev(d))

    def factor(j):
        cols = at(j * NB, NB, NB)
        t_ref[...] = x_ref[cols, cols]
        base_inverse(t_ref, n_ref)
        p = lax.dot_general(x_ref[:, cols], n_ref[...], (((1,), (1,)), ((), ())), precision=HI,
                            preferred_element_type=F32)
        bc[z, :, cols] = p[K:K + ch].astype(BF16)
        for d in zd:
            basis_copy(j, d).start()
        r = lax.broadcasted_iota(jnp.int32, (K, NB), 0)
        lk = jnp.where(r >= (j + 1) * NB, p[0:K], 0.0)

        @pl.when(j < nb - 1)
        def _():
            x_ref[...] = x_ref[...] - lax.dot_general(p, lk, (((1,), (1,)), ((), ())), precision=HI,
                                                      preferred_element_type=F32)

    def project(j):
        cols = at(j * NB, NB, NB)
        for d in zd:
            basis_copy(j, d).wait_recv()
        for t in range(NZ):
            bn[t * NB:(t + 1) * NB, cols] = bc[t, 0:NB, cols]
            bn[NZ * NB + t * ex:NZ * NB + (t + 1) * ex, cols] = bc[t, NB:ch, cols]
        for d in (2, 1, 3):
            yy = lax.rem(y + d, NY)
            ysb[d, :, cols] = jnp.dot(dz[at(yy * rows, rows, rows), :], bn[:, cols],
                                      preferred_element_type=F32).astype(BF16)
            part_copy(j, d).start()

        @pl.when(y == ysrc)
        def _():
            for d in yd:
                orth_copy(j, d).start()
            t = 4 * lax.rem(z, 2) + y
            ob[:, cols] = bn[at(t * ch, ch, 16), cols]
        proj_ref[:, cols] = jnp.dot(dz[at(y * rows, rows, rows), :], bn[:, cols], preferred_element_type=F32)

    def finish(j):
        cols = at(j * NB, NB, NB)
        for d in yd:
            part_copy(j, d).wait_recv()
        proj_ref[:, cols] += (yrb[1, :, cols].astype(F32) + yrb[2, :, cols].astype(F32) + yrb[3, :, cols].astype(F32))

        @pl.when(y != ysrc)
        def _():
            orth_copy(j, 1).wait_recv()
        orth_ref[:, cols] = ob[:, cols].astype(F32)

    def column(j, _):
        @pl.when(j == 1)
        def _():
            for c in p4[1]:
                c.wait_recv()
            for k in range(1, nb):
                n = K - k * NB
                x_ref[k * NB:K, k * NB:(k + 1) * NB] += gr[starts[k]:starts[k] + n, :]

        @pl.when(j < nb)
        def _():
            factor(j)

        @pl.when(j >= 1)
        def _():
            project(j - 1)

        @pl.when(j >= 2)
        def _():
            finish(j - 2)
        return 0
    lax.fori_loop(0, nb + 1, column, 0)
    finish(nb - 1)

    for c in done:
        c.wait_send()

    def drain(j, _):
        for d in zd:
            basis_copy(j, d).wait_send()
        for d in yd:
            part_copy(j, d).wait_send()

        @pl.when(y == ysrc)
        def _():
            for d in yd:
                orth_copy(j, d).wait_send()
        return 0
    lax.fori_loop(0, nb, drain, 0)


def basis_project_kernel(s, wz):
    ch, K = s.shape
    rr, cw = wz.shape
    rows = rr // NY
    V = pl.BlockSpec(memory_space=pltpu.VMEM)
    DM = pltpu.SemaphoreType.DMA
    M = pltpu.VMEM
    (_, n0), (_, n1) = GROUPS
    q0, q1 = n0 // NY, n1 // NY
    nb = K // NB
    return pl.pallas_call(
        basis_body,
        out_shape=(jax.ShapeDtypeStruct((ch, K), F32), jax.ShapeDtypeStruct((rows, K), F32)),
        in_specs=[V, V], out_specs=(V, V),
        scratch_shapes=[M((STACK, NB), F32), M((STACK, NB), F32), M((NY, q0, NB), F32), M((NY, q1, NB), F32),
                        M((q0, NB), F32), M((q1, NB), F32), M((NZ, q0 // NZ, NB), F32), M((NZ, q1 // NZ, NB), F32),
                        M((q0, NB), F32), M((q1, NB), F32),
                        M((rr // 2, cw), BF16), M((rr // 2, cw), BF16), M((NX, rr // 2 // NX, cw), BF16),
                        M((rr, cw), BF16), M((rr, cw), BF16), M((K + ch, K), F32), M((NB, NB), F32), M((NB, NB), F32),
                        M((NZ, ch, K), BF16), M((cw, K), BF16), M((NY, rows, K), BF16), M((NY, rows, K), BF16), M((ch, K), BF16),
                        DM((1,)), DM((1,)), DM((4,)), DM((4,)), DM((4,)), DM((4,)), DM((1,)), DM((1,)),
                        DM((2, 4)), DM((2, 4)), DM((2, 8)), DM((2, 8)), DM((2, 8)), DM((2, 8)), DM((2, 4)), DM((2, 4)),
                        DM((nb, 8)), DM((nb, 8)), DM((nb, 4)), DM((nb, 4)), DM((nb, 4)), DM((nb,))],
        compiler_params=pltpu.CompilerParams(collective_id=1, has_side_effects=True, vmem_limit_bytes=56 * 2**20),
        name="basis_project",
    )(s, wz)


def on_device(weights, gaussian):
    sketch, exchanged = sketch_kernel(weights[0], gaussian)
    orthonormal, projection = basis_project_kernel(sketch, exchanged)
    return (orthonormal[None], projection[None])


def solution(mesh):
    in_specs = (P("expert", "fsdp", None), P("fsdp", None))
    out_specs = (P("expert", "fsdp", None), P("expert", "fsdp", None))
    return jax.shard_map(
        on_device, mesh=mesh, in_specs=in_specs, out_specs=out_specs, check_vma=False
    )
```

```python
import jax
import jax.numpy as jnp
from jax import lax
from jax.sharding import PartitionSpec as P
from jax.experimental import pallas as pl
from jax.experimental.pallas import tpu as pltpu

MESH = pl.DeviceIdType.MESH
NX, NY, NZ = 4, 4, 8
NB = 128
F32, BF16 = jnp.float32, jnp.bfloat16
HI = lax.Precision.HIGHEST
SUBS = ((0, 256), (256, 640))
GROUPS = ((0, 256), (256, 512), (768, 512), (1280, 768))
STACK = 2048
AHEAD = 3
YD = (1, 3, 2)
ZD = (1, 7, 2, 6, 3, 5, 4)


def rc(src, dst, ss, rs, dev):
    return pltpu.make_async_remote_copy(src_ref=src, dst_ref=dst, send_sem=ss, recv_sem=rs, device_id=dev,
                                        device_id_type=MESH)


def at(start, size, unit):
    return pl.ds(pl.multiple_of(start, unit), size)


def base_inverse(t_ref, n_ref):
    sub = lax.broadcasted_iota(jnp.int32, (8, NB), 0)
    row = lax.broadcasted_iota(jnp.int32, (NB, NB), 0)
    col = lax.broadcasted_iota(jnp.int32, (NB, NB), 1)
    n_ref[...] = jnp.where(row == col, 1.0, 0.0).astype(F32)
    nsub = NB // 8
    wide = lambda v: jnp.broadcast_to(v, (8, NB))
    cur_t, cur_n = t_ref[0:8, :], n_ref[0:8, :]
    for b in range(nsub):
        r0 = 8 * b
        last = b == nsub - 1
        c = [wide(cur_t[:, r0 + i:r0 + i + 1]) for i in range(8)]
        if not last:
            nt, nn = t_ref[r0 + 8:r0 + 16, :], n_ref[r0 + 8:r0 + 16, :]
            d = [wide(nt[:, r0 + i:r0 + i + 1]) for i in range(8)]
        for i in range(8):
            rs = lax.rsqrt(wide(c[i][i:i + 1, :]))
            m = c[i] * rs
            mk = {}
            for k in range(i + 1, 8):
                mk[k] = wide(m[k:k + 1, :])
                c[k] = c[k] - m * mk[k]
            mm = jnp.where(sub > i, m, 0.0)
            ft = wide(cur_t[i:i + 1, :]) * rs
            fn = wide(cur_n[i:i + 1, :]) * rs
            cur_t = jnp.where(sub == i, ft, cur_t - mm * ft)
            cur_n = jnp.where(sub == i, fn, cur_n - mm * fn)
            if not last:
                md = d[i] * rs
                for k in range(i + 1, 8):
                    d[k] = d[k] - md * mk[k]
                nt = nt - md * ft
                nn = nn - md * fn
        n_ref[r0:r0 + 8, :] = cur_n
        if not last:
            if b < nsub - 2:
                both = jnp.concatenate([cur_t, cur_n], axis=1)
                upd = lax.dot_general(cur_t, both, (((0,), (0,)), ((), ())), precision=HI, preferred_element_type=F32)
                t_ref[r0 + 16:, :] = t_ref[r0 + 16:, :] - upd[r0 + 16:, :NB]
                n_ref[r0 + 16:, :] = n_ref[r0 + 16:, :] - upd[r0 + 16:, NB:]
            cur_t, cur_n = nt, nn


def body(w_ref, g_ref, out_ref,
         wv, gv, p_ref, sbuf, rbuf, sp, sx, tb, tr, mo, mr, s_ref,
         gp, gr, yrv, ybv, zrv, qfv,
         fw, fb, fr, mw, dz, x_ref, l_ref, ln_ref, t_ref, bc, bn, ysb, yrb, ob,
         wsend, wrecv, gsend, grecv, gxsend, gxrecv, fsend, frecv, zsend, zrecv, csend, crecv, xsend, xrecv, hsend, hrecv,
         loc, f1s, f1r, f2s, f2r, f3s, f3r, f4s, f4r, ys1, yr1, zs1, zr1, zs2, zr2, ys2, yr2, bs, br, ps, pr, os_, or_):
    rows, D = w_ref.shape
    K = g_ref.shape[1]
    cw = D // NY
    ch = cw // NZ
    ex = ch - NB
    rr = rows * NY
    nb = K // NB
    e = lax.axis_index("expert")
    f = lax.axis_index("fsdp")
    x, core, y, z = e // 2, lax.rem(e, 2), lax.rem(f, NY), f // NY
    xdev = lambda d: (lax.rem(x + d, NX) * 2 + core, f)
    ydev = lambda d: (e, z * NY + lax.rem(y + d, NY))
    zdev = lambda d: (e, lax.rem(z + d, NZ) * NY + y)
    sib = (e + 1 - 2 * core, f)

    lg = pltpu.make_async_copy(g_ref, gv.at[at(y * rows, rows, rows), :], loc.at[0])
    lg.start()
    barrier = pltpu.get_barrier_semaphore()
    partners = [ydev(d) for d in YD] + [zdev(d) for d in ZD] + [xdev(d) for d in YD] + [sib]
    for p in partners:
        pl.semaphore_signal(barrier, inc=1, device_id=p, device_id_type=MESH)
    pl.semaphore_wait(barrier, len(partners))

    hr, qr = rows // 2, rows // 8
    mine = at(y * rows, rows, rows)
    mypart = core * hr + x * qr
    done = []
    gcs = []
    for d in YD:
        c = rc(g_ref.at[at(mypart, qr, qr), :], gv.at[at(y * rows + mypart, qr, qr), :], gsend.at[d], grecv.at[d], ydev(d))
        c.start()
        gcs.append(c)
    seq = [NZ] + [lax.rem(z + k, NZ) for k in (4, 3, 5, 2, 6, 1, 7, 0)]
    wcs, lws = [], []
    for k, b in enumerate(seq):
        lw = pltpu.make_async_copy(w_ref.at[:, at(y * cw + b * NB, NB, NB)], wv.at[mine, at(b * NB, NB, NB)], loc.at[1 + k])
        lw.start()
        lws.append(lw)
        now = []
        for d in YD:
            yy = lax.rem(y + d, NY)
            c = rc(w_ref.at[:, at(yy * cw + b * NB, NB, NB)], wv.at[mine, at(b * NB, NB, NB)],
                   wsend.at[k, d], wrecv.at[k, d], ydev(d))
            c.start()
            now.append(c)
        wcs.append(now)
    gxs = []
    for i, d in enumerate(YD):
        gcs[i].wait_recv()
        piece = at(lax.rem(y - d + NY, NY) * rows + mypart, qr, qr)
        for dx in YD:
            c = rc(gv.at[piece, :], gv.at[piece, :], gxsend.at[d, dx], gxrecv.at[d, dx], xdev(dx))
            c.start()
            gxs.append(c)
    fcs = []
    for i, d in enumerate(YD):
        for c in gxs[3 * i:3 * i + 3]:
            c.wait_recv()
        piece = at(lax.rem(y - d + NY, NY) * rows + core * hr, hr, hr)
        c = rc(gv.at[piece, :], gv.at[piece, :], fsend.at[d], frecv.at[d], sib)
        c.start()
        fcs.append(c)
    lg.wait()
    for c in fcs:
        c.wait_recv()

    def product(k):
        lws[k].wait()
        for c in wcs[k]:
            c.wait_recv()
        o = at(seq[k] * NB, NB, NB)
        p_ref[o, :] = lax.dot_general(wv[:, o], gv[...], (((0,), (0,)), ((), ())), preferred_element_type=F32)

    ha = 64
    prev = {}

    def own(t, r, n, c0, c1):
        head = p_ref[at(t * NB + r, min(n, NB - r), 16), c0:c1]
        if r + n <= NB:
            return head
        return jnp.concatenate([head, p_ref[at(NZ * NB + t * ex, ex, 16), c0:c1]], axis=0)

    product(0)
    for s in range(4):
        for k in ((1,), (2, 3), (4, 5), (6, 7))[s]:
            product(k)
        for u, (c0, c1) in enumerate(SUBS):
            for dr, d in ((0, 1), (1, NZ - 1)):
                t = lax.rem(z + (4 - s if dr == 0 else NZ - 4 + s), NZ)
                a, m = (0, ha) if dr == 0 else (ha, ch - ha)
                q, l = (ha, ch - ha) if dr == 0 else (0, ha)
                if s:
                    prev[dr, u].wait_recv()
                if s == 0:
                    sbuf[dr, s, a:a + m, c0:c1] = own(t, a, m, c0, c1).astype(BF16)
                    r, n = a, m
                elif s == 1:
                    sbuf[dr, s, a:a + m, c0:c1] = (own(t, a, m, c0, c1) + rbuf[dr, 0, a:a + m, c0:c1].astype(F32)).astype(BF16)
                    sbuf[dr, s, q:q + l, c0:c1] = own(t, q, l, c0, c1).astype(BF16)
                    r, n = 0, ch
                else:
                    sbuf[dr, s, :, c0:c1] = (own(t, 0, ch, c0, c1) + rbuf[dr, s - 1, :, c0:c1].astype(F32)).astype(BF16)
                    r, n = 0, ch
                c = rc(sbuf.at[dr, s, pl.ds(r, n), pl.ds(c0, c1 - c0)], rbuf.at[dr, s, pl.ds(r, n), pl.ds(c0, c1 - c0)],
                       zsend.at[dr, s, u], zrecv.at[dr, s, u], zdev(d))
                c.start()
                done.append(c)
                prev[dr, u] = c
    product(8)
    hm = 80
    half = at((ch - hm) * core, hm, 16)
    rest = at(hm * (1 - core), ch - hm, 16)
    pairs = []
    for u, (c0, c1) in enumerate(SUBS):
        prev[0, u].wait_recv()
        prev[1, u].wait_recv()
        sp[:, c0:c1] = (own(z, 0, ch, c0, c1) + rbuf[0, 3, :, c0:c1].astype(F32) + rbuf[1, 3, :, c0:c1].astype(F32))
        c = rc(sp.at[:, pl.ds(c0, c1 - c0)], sx.at[:, pl.ds(c0, c1 - c0)], csend.at[u], crecv.at[u], sib)
        c.start()
        pairs.append(c)
    hf = rr // 2
    f1 = rc(wv.at[at(hf * (1 - core), hf, hf), :], fw, f1s.at[0], f1r.at[0], sib)
    xs = []
    for u, (c0, c1) in enumerate(SUBS):
        pairs[u].wait_recv()
        mo[:, c0:c1] = sp[half, c0:c1] + sx[half, c0:c1]
        tb[:, c0:c1] = mo[:, c0:c1].astype(BF16)
        now = []
        for d in YD:
            c = rc(tb.at[:, pl.ds(c0, c1 - c0)], tr.at[d, :, pl.ds(c0, c1 - c0)], xsend.at[u, d], xrecv.at[u, d], xdev(d))
            c.start()
            now.append(c)
        xs.append(now)
    f1.start()
    hs = []
    for u, (c0, c1) in enumerate(SUBS):
        for c in xs[u]:
            c.wait_recv()
        mo[:, c0:c1] = (mo[:, c0:c1] + tr[1, :, c0:c1].astype(F32) + tr[2, :, c0:c1].astype(F32)
                        + tr[3, :, c0:c1].astype(F32)) * (1.0 / (2 * NX))
        c = rc(mo.at[:, pl.ds(c0, c1 - c0)], mr.at[:, pl.ds(c0, c1 - c0)], hsend.at[u], hrecv.at[u], sib)
        c.start()
        hs.append(c)
        s_ref[half, c0:c1] = sp[half, c0:c1] - mo[:, c0:c1]

    def sketch_rest(u):
        c0, c1 = SUBS[u]
        hs[u].wait_recv()
        s_ref[rest, c0:c1] = sp[rest, c0:c1] - mr[at((2 * hm - ch) * (1 - core), ch - hm, 16), c0:c1]

    starts = [sum(K - i * NB for i in range(j)) for j in range(nb)]

    def gram(j, i0, i1):
        gp[starts[j] + (i0 - j) * NB:starts[j] + (i1 - j) * NB, :] = lax.dot_general(
            s_ref[:, i0 * NB:i1 * NB], s_ref[:, j * NB:(j + 1) * NB], (((0,), (0,)), ((), ())),
            precision=HI, preferred_element_type=F32)

    def copies(phase, g):
        a, n = GROUPS[g]
        q, m = n // NY, n // NY // NZ
        if phase == 1:
            return [rc(gp.at[at(a + q * lax.rem(y + d, NY), q, 8), :], yrv[g].at[d], ys1.at[g, d], yr1.at[g, d], ydev(d))
                    for d in YD]
        if phase == 2:
            return [rc(ybv[g].at[at(m * lax.rem(z + d, NZ), m, 8), :], zrv[g].at[d], zs1.at[g, d], zr1.at[g, d], zdev(d))
                    for d in ZD]
        if phase == 3:
            here = at(m * z, m, 8)
            return [rc(qfv[g].at[here, :], qfv[g].at[here, :], zs2.at[g, d], zr2.at[g, d], zdev(d)) for d in ZD]
        here = at(a + q * y, q, 8)
        return [rc(qfv[g], gr.at[here, :], ys2.at[g, d], yr2.at[g, d], ydev(d)) for d in YD]

    def send(phase, g):
        for c in copies(phase, g):
            c.start()

    def receive(phase, g):
        for c in copies(phase, g):
            c.wait_recv()

    def phase2(g):
        a, n = GROUPS[g]
        q = n // NY
        receive(1, g)
        ybv[g][...] = gp[at(a + q * y, q, 8), :] + yrv[g][1] + yrv[g][2] + yrv[g][3]
        send(2, g)

    def phase3(g):
        m = GROUPS[g][1] // NY // NZ
        receive(2, g)
        here = at(m * z, m, 8)
        tot = ybv[g][here, :]
        for d in range(1, NZ):
            tot = tot + zrv[g][d]
        qfv[g][here, :] = tot * (1.0 / D)
        send(3, g)

    def phase4(g):
        a, n = GROUPS[g]
        q = n // NY
        receive(3, g)
        send(4, g)
        gr[at(a + q * y, q, 8), :] = qfv[g][...]

    def basis_copy(j, d):
        cols = at(j * NB, NB, NB)
        return rc(bc.at[z, :, cols], bc.at[z, :, cols], bs.at[j, d], br.at[j, d], zdev(d))

    def send_column(j, ref, r0):
        cols = at(j * NB, NB, NB)
        bc[z, :, cols] = ref[r0:r0 + ch, cols].astype(BF16)
        for d in ZD:
            basis_copy(j, d).start()

    sketch_rest(0)
    gram(0, 0, 2)
    send(1, 0)
    send_column(0, s_ref, 0)
    sketch_rest(1)
    gram(0, 2, nb)
    gram(1, 1, nb)
    send(1, 1)
    gram(2, 2, nb)
    send(1, 2)
    gram(3, 3, nb)
    gram(4, 4, nb)
    gp[starts[4] + NB:, :] = jnp.zeros((STACK - starts[4] - NB, NB), F32)
    send(1, 3)
    phase2(0)
    f1.wait_recv()
    step = 64

    def pair(i, _):
        o = at(i * step, step, step)
        fb[o, :] = (wv[at(hf * core + i * step, step, step), :].astype(F32) + fw[o, :].astype(F32)).astype(BF16)
        return 0
    lax.fori_loop(0, hf // step, pair, 0)
    qx = hf // NX
    f2 = [rc(fb.at[at(qx * lax.rem(x + d, NX), qx, qx), :], fr.at[d], f2s.at[d], f2r.at[d], xdev(d)) for d in YD]
    for c in f2:
        c.start()
    phase2(1)
    phase2(2)
    phase3(0)
    phase2(3)
    phase3(1)
    x_ref[0:K, :] = jnp.zeros((K, K), F32)
    x_ref[K:K + ch, :] = s_ref[...]
    l_ref[...] = jnp.zeros((K, K), F32)
    out_ref[...] = jnp.zeros(out_ref.shape, F32)
    phase4(0)
    phase3(2)
    send_column(1, s_ref, 0)
    phase4(1)
    for c in f2:
        c.wait_recv()

    def four(i, _):
        o = at(i * 32, 32, 32)
        mw[at(hf * core + qx * x + i * 32, 32, 32), :] = (
            fb[at(qx * x + i * 32, 32, 32), :].astype(F32) + fr[1, o, :].astype(F32) + fr[2, o, :].astype(F32)
            + fr[3, o, :].astype(F32)).astype(BF16)
        return 0
    lax.fori_loop(0, qx // 32, four, 0)
    part = at(hf * core + qx * x, qx, qx)
    f3 = [rc(mw.at[part, :], mw.at[part, :], f3s.at[d], f3r.at[d], xdev(d)) for d in YD]
    for c in f3:
        c.start()
    phase3(3)
    send_column(2, s_ref, 0)
    receive(4, 0)
    x_ref[0:2 * NB, 0:NB] = gr[0:2 * NB, :]

    halfrows = at(hf * core, hf, hf)
    f4 = rc(mw.at[halfrows, :], mw.at[halfrows, :], f4s.at[0], f4r.at[0], sib)
    ysrc = z // 2

    def part_copy(j, d):
        cols = at(j * NB, NB, NB)
        return rc(ysb.at[d, :, cols], yrb.at[d, :, cols], ps.at[j, d], pr.at[j, d], ydev(d))

    def orth_copy(j, d):
        cols = at(j * NB, NB, NB)
        t = 4 * lax.rem(z, 2) + lax.rem(y + d, NY)
        return rc(bn.at[at(t * ch, ch, 16), cols], ob.at[:, cols], os_.at[j, d], or_.at[j], ydev(d))

    def factor(j):
        cols = at(j * NB, NB, NB)
        n_ref = ln_ref.at[j]
        t_ref[...] = x_ref[cols, cols]
        base_inverse(t_ref, n_ref)

        @pl.when(j == 0)
        def _():
            phase4(2)
            receive(4, 1)
            x_ref[2 * NB:K, 0:NB] = gr[2 * NB:K, :]
        p = lax.dot_general(x_ref[:, cols], n_ref[...], (((1,), (1,)), ((), ())), precision=HI,
                            preferred_element_type=F32)
        r = lax.broadcasted_iota(jnp.int32, (K, NB), 0)
        l_ref[:, cols] = jnp.where(r >= (j + 1) * NB, p[0:K], 0.0)

        @pl.when(j < nb - 1)
        def _():
            x_ref[...] = x_ref[...] - lax.dot_general(p, l_ref[:, cols], (((1,), (1,)), ((), ())), precision=HI,
                                                      preferred_element_type=F32)

        @pl.when(j < nb - AHEAD)
        def _():
            send_column(j + AHEAD, x_ref, K)

    def project(j):
        cols = at(j * NB, NB, NB)
        for d in ZD:
            basis_copy(j, d).wait_recv()
        for t in range(NZ):
            bn[t * NB:(t + 1) * NB, cols] = bc[t, 0:NB, cols]
            bn[NZ * NB + t * ex:NZ * NB + (t + 1) * ex, cols] = bc[t, NB:ch, cols]
        for d in (2, 1, 3):
            ysb[d, :, cols] = jnp.dot(dz[at(lax.rem(y + d, NY) * rows, rows, rows), :], bn[:, cols],
                                      preferred_element_type=F32).astype(BF16)
            part_copy(j, d).start()

        @pl.when(y == ysrc)
        def _():
            for d in YD:
                orth_copy(j, d).start()
            t = 4 * lax.rem(z, 2) + y
            ob[:, cols] = bn[at(t * ch, ch, 16), cols]
        out_ref[ch:, cols] = jnp.dot(dz[mine, :], bn[:, cols], preferred_element_type=F32)

    def finish(j):
        cols = at(j * NB, NB, NB)
        for d in YD:
            part_copy(j, d).wait_recv()

        @pl.when(y != ysrc)
        def _():
            orth_copy(j, 1).wait_recv()
        q = out_ref[ch:, cols] + (yrb[1, :, cols].astype(F32) + yrb[2, :, cols].astype(F32) + yrb[3, :, cols].astype(F32))
        col = lax.broadcasted_iota(jnp.int32, (NB, K), 1)
        first = jnp.maximum(j - AHEAD + 1, 0) * NB
        lrow = jnp.where((col >= first) & (col < j * NB), l_ref[cols, :], 0.0)
        prior = jnp.where(lax.broadcasted_iota(jnp.int32, out_ref.shape, 1) < j * NB, out_ref[...], 0.0)
        both = jnp.concatenate([ob[:, cols].astype(F32), q], axis=0) - lax.dot_general(
            prior, lrow, (((1,), (1,)), ((), ())), precision=HI, preferred_element_type=F32)
        out_ref[:, cols] = lax.dot_general(both, ln_ref[j], (((1,), (1,)), ((), ())), precision=HI,
                                           preferred_element_type=F32)

    def column(j, _):
        @pl.when(j == 1)
        def _():
            phase4(3)
            for c in f3:
                c.wait_recv()
            f4.start()
            receive(4, 2)
            n = K - NB
            x_ref[NB:K, NB:2 * NB] += gr[starts[1]:starts[1] + n, :]
            x_ref[2 * NB:3 * NB, 2 * NB:3 * NB] += gr[starts[2]:starts[2] + NB, :]
            f4.wait_recv()

            def delta(i, _):
                o = at(i * step, step, step)
                dz[o, :] = (wv[o, :].astype(F32) - mw[o, :].astype(F32) * (1.0 / (2 * NX))).astype(BF16)
                return 0
            lax.fori_loop(0, rr // step, delta, 0)
            project(0)

        @pl.when(j == 2)
        def _():
            receive(4, 3)
            x_ref[3 * NB:K, 2 * NB:3 * NB] += gr[starts[2] + NB:starts[3], :]
            x_ref[3 * NB:K, 3 * NB:4 * NB] += gr[starts[3]:starts[4], :]
            x_ref[4 * NB:K, 4 * NB:5 * NB] += gr[starts[4]:starts[4] + NB, :]
            project(1)

        @pl.when(j >= 2)
        def _():
            project(j)
        factor(j)

        @pl.when(j == 1)
        def _():
            finish(0)

        @pl.when(j == 2)
        def _():
            finish(1)

        @pl.when(j >= 2)
        def _():
            finish(j)
        return 0
    lax.fori_loop(0, nb, column, 0)

    done += gcs + gxs + fcs + [c for now in wcs + xs for c in now] + pairs + hs + [f1, f4] + f2 + f3
    for c in done + [c for phase in (1, 2, 3, 4) for g in range(len(GROUPS)) for c in copies(phase, g)]:
        c.wait_send()

    def drain(j, _):
        for d in ZD:
            basis_copy(j, d).wait_send()
        for d in YD:
            part_copy(j, d).wait_send()

        @pl.when(y == ysrc)
        def _():
            for d in YD:
                orth_copy(j, d).wait_send()
        return 0
    lax.fori_loop(0, nb, drain, 0)


def compress(w, g):
    rows, D = w.shape
    K = g.shape[1]
    cw = D // NY
    ch = cw // NZ
    rr = rows * NY
    nb = K // NB
    nu = len(SUBS)
    ng = len(GROUPS)
    V = pl.BlockSpec(memory_space=pltpu.VMEM)
    A = pl.BlockSpec(memory_space=pl.ANY)
    DM = pltpu.SemaphoreType.DMA
    M = pltpu.VMEM
    quarter = [n // NY for _, n in GROUPS]
    return pl.pallas_call(
        body,
        out_shape=jax.ShapeDtypeStruct((ch + rows, K), F32),
        in_specs=[A, A], out_specs=V,
        scratch_shapes=[
            M((rr, cw), BF16), M((rr, K), BF16), M((cw, K), F32), M((2, 4, ch, K), BF16), M((2, 4, ch, K), BF16),
            M((ch, K), F32), M((ch, K), F32), M((80, K), BF16), M((4, 80, K), BF16), M((80, K), F32), M((80, K), F32),
            M((ch, K), F32),
            M((STACK, NB), F32), M((STACK, NB), F32), [M((NY, q, NB), F32) for q in quarter], [M((q, NB), F32) for q in quarter],
            [M((NZ, q // NZ, NB), F32) for q in quarter], [M((q, NB), F32) for q in quarter],
            M((rr // 2, cw), BF16), M((rr // 2, cw), BF16), M((NX, rr // 2 // NX, cw), BF16), M((rr, cw), BF16), M((rr, cw), BF16),
            M((K + ch, K), F32), M((K, K), F32), M((nb, NB, NB), F32), M((NB, NB), F32),
            M((NZ, ch, K), BF16), M((cw, K), BF16), M((NY, rows, K), BF16), M((NY, rows, K), BF16), M((ch, K), BF16),
            DM((9, 4)), DM((9, 4)), DM((4,)), DM((4,)), DM((4, 4)), DM((4, 4)), DM((4,)), DM((4,)),
            DM((2, 4, nu)), DM((2, 4, nu)), DM((nu,)), DM((nu,)), DM((nu, 4)), DM((nu, 4)), DM((nu,)), DM((nu,)),
            DM((10,)), DM((1,)), DM((1,)), DM((4,)), DM((4,)), DM((4,)), DM((4,)), DM((1,)), DM((1,)),
            DM((ng, 4)), DM((ng, 4)), DM((ng, 8)), DM((ng, 8)), DM((ng, 8)), DM((ng, 8)), DM((ng, 4)), DM((ng, 4)),
            DM((nb, 8)), DM((nb, 8)), DM((nb, 4)), DM((nb, 4)), DM((nb, 4)), DM((nb,))],
        compiler_params=pltpu.CompilerParams(collective_id=0, has_side_effects=True, vmem_limit_bytes=60 * 2**20),
        name="delta_compress",
    )(w, g)


def on_device(weights, gaussian):
    both = compress(weights[0], gaussian)
    ch = both.shape[0] - weights.shape[1]
    return (both[None, :ch], both[None, ch:])


def solution(mesh):
    in_specs = (P("expert", "fsdp", None), P("fsdp", None))
    out_specs = (P("expert", "fsdp", None), P("expert", "fsdp", None))
    return jax.shard_map(
        on_device, mesh=mesh, in_specs=in_specs, out_specs=out_specs, check_vma=False
    )
```

```python
import jax
import jax.numpy as jnp
from jax import lax
from jax.sharding import PartitionSpec as P
from jax.experimental import pallas as pl
from jax.experimental.pallas import tpu as pltpu

MESH = pl.DeviceIdType.MESH
NX, NY, NZ = 4, 4, 8
NB = 128
F32, BF16 = jnp.float32, jnp.bfloat16
HI = lax.Precision.HIGHEST
SUBS = ((0, 256), (256, 640))
GROUPS = ((0, 256), (256, 512), (768, 512), (1280, 768))
STACK = 2048
AHEAD = 3
PW = 64
YD = (1, 3, 2)
ZD = (1, 7, 2, 6, 3, 5, 4)


def rc(src, dst, ss, rs, dev):
    return pltpu.make_async_remote_copy(src_ref=src, dst_ref=dst, send_sem=ss, recv_sem=rs, device_id=dev,
                                        device_id_type=MESH)


def at(start, size, unit):
    return pl.ds(pl.multiple_of(start, unit), size)


def wide(v):
    return jnp.broadcast_to(v, (8, NB))


def base_inverse(t_ref, n_ref):
    sub = lax.broadcasted_iota(jnp.int32, (8, NB), 0)
    row = lax.broadcasted_iota(jnp.int32, (NB, NB), 0)
    col = lax.broadcasted_iota(jnp.int32, (NB, NB), 1)
    n_ref[...] = jnp.where(row == col, 1.0, 0.0).astype(F32)
    npan = PW // 8
    for p0 in range(0, NB, PW):
        rt_ = [t_ref[p0 + 8 * s:p0 + 8 * s + 8, :] for s in range(npan)]
        rn_ = [n_ref[p0 + 8 * s:p0 + 8 * s + 8, :] for s in range(npan)]
        c = [wide(rt_[0][:, p0 + i:p0 + i + 1]) for i in range(8)]
        for b in range(npan):
            r0 = p0 + 8 * b
            a = {(k, i): wide(c[i][k:k + 1, :]) for i in range(8) for k in range(i, 8)}
            later = range(b + 1, npan)
            dd = {s: [wide(rt_[s][:, r0 + i:r0 + i + 1]) for i in range(8)] for s in later}
            if b + 1 < npan:
                e = [wide(rt_[b + 1][:, r0 + 8 + i:r0 + 9 + i]) for i in range(8)]
            l = {}
            rs = []
            for i in range(8):
                r = lax.rsqrt(a[i, i])
                rs.append(r)
                for k in range(i + 1, 8):
                    l[k, i] = a[k, i] * r
                for k in range(i + 1, 8):
                    for k2 in range(k, 8):
                        a[k2, k] = a[k2, k] - l[k2, i] * l[k, i]
            rt = [wide(rt_[b][i:i + 1, :]) for i in range(8)]
            rn = [wide(rn_[b][i:i + 1, :]) for i in range(8)]
            for i in range(8):
                rt[i] = rt[i] * rs[i]
                rn[i] = rn[i] * rs[i]
                for k in range(i + 1, 8):
                    rt[k] = rt[k] - l[k, i] * rt[i]
                    rn[k] = rn[k] - l[k, i] * rn[i]
            for s in later:
                d = dd[s]
                for i in range(8):
                    v = d[i] * rs[i]
                    for k in range(i + 1, 8):
                        d[k] = d[k] - v * l[k, i]
                    rt_[s] = rt_[s] - v * rt[i]
                    rn_[s] = rn_[s] - v * rn[i]
                    if s == b + 1:
                        for k in range(8):
                            e[k] = e[k] - v * wide(v[k:k + 1, :])
            ct, cn = rt[0], rn[0]
            for i in range(1, 8):
                ct = jnp.where(sub == i, rt[i], ct)
                cn = jnp.where(sub == i, rn[i], cn)
            rt_[b], rn_[b] = ct, cn
            n_ref[r0:r0 + 8, :] = cn
            if b + 1 < npan:
                c = e
        q0 = p0 + PW
        if q0 < NB:
            lt = jnp.concatenate(rt_, axis=0)
            both = jnp.concatenate([lt, jnp.concatenate(rn_, axis=0)], axis=1)
            upd = lax.dot_general(lt, both, (((0,), (0,)), ((), ())), precision=HI, preferred_element_type=F32)
            t_ref[q0:, :] = t_ref[q0:, :] - upd[q0:, :NB]
            n_ref[q0:, :] = n_ref[q0:, :] - upd[q0:, NB:]


def body(w_ref, g_ref, out_ref,
         wv, gv, p_ref, sbuf, rbuf, sp, sx, tb, tr, mo, mr, s_ref,
         gp, gr, yrv, ybv, zrv, qfv,
         fw, fb, fr, mw, dz, x_ref, l_ref, ln_ref, t_ref, bc, bn, ysb, yrb, ob,
         wsend, wrecv, gsend, grecv, gxsend, gxrecv, fsend, frecv, zsend, zrecv, csend, crecv, xsend, xrecv, hsend, hrecv,
         loc, f1s, f1r, f2s, f2r, f3s, f3r, f4s, f4r, ys1, yr1, zs1, zr1, zs2, zr2, ys2, yr2, bs, br, ps, pr, os_, or_):
    rows, D = w_ref.shape
    K = g_ref.shape[1]
    cw = D // NY
    ch = cw // NZ
    ex = ch - NB
    rr = rows * NY
    nb = K // NB
    e = lax.axis_index("expert")
    f = lax.axis_index("fsdp")
    x, core, y, z = e // 2, lax.rem(e, 2), lax.rem(f, NY), f // NY
    xdev = lambda d: (lax.rem(x + d, NX) * 2 + core, f)
    ydev = lambda d: (e, z * NY + lax.rem(y + d, NY))
    zdev = lambda d: (e, lax.rem(z + d, NZ) * NY + y)
    sib = (e + 1 - 2 * core, f)

    lg = pltpu.make_async_copy(g_ref, gv.at[at(y * rows, rows, rows), :], loc.at[0])
    lg.start()
    barrier = pltpu.get_barrier_semaphore()
    partners = [ydev(d) for d in YD] + [zdev(d) for d in ZD] + [xdev(d) for d in YD] + [sib]
    for p in partners:
        pl.semaphore_signal(barrier, inc=1, device_id=p, device_id_type=MESH)
    pl.semaphore_wait(barrier, len(partners))

    hr, qr = rows // 2, rows // 8
    mine = at(y * rows, rows, rows)
    mypart = core * hr + x * qr
    done = []
    gcs = []
    for d in YD:
        c = rc(g_ref.at[at(mypart, qr, qr), :], gv.at[at(y * rows + mypart, qr, qr), :], gsend.at[d], grecv.at[d], ydev(d))
        c.start()
        gcs.append(c)
    seq = [NZ] + [lax.rem(z + k, NZ) for k in (4, 3, 5, 2, 6, 1, 7, 0)]
    wcs, lws = [], []
    for k, b in enumerate(seq):
        lw = pltpu.make_async_copy(w_ref.at[:, at(y * cw + b * NB, NB, NB)], wv.at[mine, at(b * NB, NB, NB)], loc.at[1 + k])
        lw.start()
        lws.append(lw)
        now = []
        for d in YD:
            yy = lax.rem(y + d, NY)
            c = rc(w_ref.at[:, at(yy * cw + b * NB, NB, NB)], wv.at[mine, at(b * NB, NB, NB)],
                   wsend.at[k, d], wrecv.at[k, d], ydev(d))
            c.start()
            now.append(c)
        wcs.append(now)
    gxs = []
    for i, d in enumerate(YD):
        gcs[i].wait_recv()
        piece = at(lax.rem(y - d + NY, NY) * rows + mypart, qr, qr)
        for dx in YD:
            c = rc(gv.at[piece, :], gv.at[piece, :], gxsend.at[d, dx], gxrecv.at[d, dx], xdev(dx))
            c.start()
            gxs.append(c)
    fcs = []
    for i, d in enumerate(YD):
        for c in gxs[3 * i:3 * i + 3]:
            c.wait_recv()
        piece = at(lax.rem(y - d + NY, NY) * rows + core * hr, hr, hr)
        c = rc(gv.at[piece, :], gv.at[piece, :], fsend.at[d], frecv.at[d], sib)
        c.start()
        fcs.append(c)
    lg.wait()
    for c in fcs:
        c.wait_recv()

    def product(k):
        lws[k].wait()
        for c in wcs[k]:
            c.wait_recv()
        o = at(seq[k] * NB, NB, NB)
        p_ref[o, :] = lax.dot_general(wv[:, o], gv[...], (((0,), (0,)), ((), ())), preferred_element_type=F32)

    ha = 64
    prev = {}

    def own(t, r, n, c0, c1):
        head = p_ref[at(t * NB + r, min(n, NB - r), 16), c0:c1]
        if r + n <= NB:
            return head
        return jnp.concatenate([head, p_ref[at(NZ * NB + t * ex, ex, 16), c0:c1]], axis=0)

    product(0)
    for s in range(4):
        for k in ((1,), (2, 3), (4, 5), (6, 7))[s]:
            product(k)
        for u, (c0, c1) in enumerate(SUBS):
            for dr, d in ((0, 1), (1, NZ - 1)):
                t = lax.rem(z + (4 - s if dr == 0 else NZ - 4 + s), NZ)
                a, m = (0, ha) if dr == 0 else (ha, ch - ha)
                q, l = (ha, ch - ha) if dr == 0 else (0, ha)
                if s:
                    prev[dr, u].wait_recv()
                if s == 0:
                    sbuf[dr, s, a:a + m, c0:c1] = own(t, a, m, c0, c1).astype(BF16)
                    r, n = a, m
                elif s == 1:
                    sbuf[dr, s, a:a + m, c0:c1] = (own(t, a, m, c0, c1) + rbuf[dr, 0, a:a + m, c0:c1].astype(F32)).astype(BF16)
                    sbuf[dr, s, q:q + l, c0:c1] = own(t, q, l, c0, c1).astype(BF16)
                    r, n = 0, ch
                else:
                    sbuf[dr, s, :, c0:c1] = (own(t, 0, ch, c0, c1) + rbuf[dr, s - 1, :, c0:c1].astype(F32)).astype(BF16)
                    r, n = 0, ch
                c = rc(sbuf.at[dr, s, pl.ds(r, n), pl.ds(c0, c1 - c0)], rbuf.at[dr, s, pl.ds(r, n), pl.ds(c0, c1 - c0)],
                       zsend.at[dr, s, u], zrecv.at[dr, s, u], zdev(d))
                c.start()
                done.append(c)
                prev[dr, u] = c
    product(8)
    hf = rr // 2
    f1 = rc(wv.at[at(hf * (1 - core), hf, hf), :], fw, f1s.at[0], f1r.at[0], sib)
    f1.start()
    hm = 80
    half = at((ch - hm) * core, hm, 16)
    rest = at(hm * (1 - core), ch - hm, 16)
    pairs = []
    for u, (c0, c1) in enumerate(SUBS):
        prev[0, u].wait_recv()
        prev[1, u].wait_recv()
        sp[:, c0:c1] = (own(z, 0, ch, c0, c1) + rbuf[0, 3, :, c0:c1].astype(F32) + rbuf[1, 3, :, c0:c1].astype(F32))
        c = rc(sp.at[:, pl.ds(c0, c1 - c0)], sx.at[:, pl.ds(c0, c1 - c0)], csend.at[u], crecv.at[u], sib)
        c.start()
        pairs.append(c)
    xs = []
    for u, (c0, c1) in enumerate(SUBS):
        pairs[u].wait_recv()
        mo[:, c0:c1] = sp[half, c0:c1] + sx[half, c0:c1]
        tb[:, c0:c1] = mo[:, c0:c1].astype(BF16)
        now = []
        for d in YD:
            c = rc(tb.at[:, pl.ds(c0, c1 - c0)], tr.at[d, :, pl.ds(c0, c1 - c0)], xsend.at[u, d], xrecv.at[u, d], xdev(d))
            c.start()
            now.append(c)
        xs.append(now)
    f1.wait_recv()
    step = 64

    def pair(i, _):
        o = at(i * step, step, step)
        fb[o, :] = (wv[at(hf * core + i * step, step, step), :].astype(F32) + fw[o, :].astype(F32)).astype(BF16)
        return 0
    lax.fori_loop(0, hf // step, pair, 0)
    qx = hf // NX
    f2 = [rc(fb.at[at(qx * lax.rem(x + d, NX), qx, qx), :], fr.at[d], f2s.at[d], f2r.at[d], xdev(d)) for d in YD]
    for c in f2:
        c.start()
    hs = []
    for u, (c0, c1) in enumerate(SUBS):
        for c in xs[u]:
            c.wait_recv()
        mo[:, c0:c1] = (mo[:, c0:c1] + tr[1, :, c0:c1].astype(F32) + tr[2, :, c0:c1].astype(F32)
                        + tr[3, :, c0:c1].astype(F32)) * (1.0 / (2 * NX))
        c = rc(mo.at[:, pl.ds(c0, c1 - c0)], mr.at[:, pl.ds(c0, c1 - c0)], hsend.at[u], hrecv.at[u], sib)
        c.start()
        hs.append(c)
        s_ref[half, c0:c1] = sp[half, c0:c1] - mo[:, c0:c1]

    def sketch_rest(u):
        c0, c1 = SUBS[u]
        hs[u].wait_recv()
        s_ref[rest, c0:c1] = sp[rest, c0:c1] - mr[at((2 * hm - ch) * (1 - core), ch - hm, 16), c0:c1]

    starts = [sum(K - i * NB for i in range(j)) for j in range(nb)]

    def gram(j, i0, i1):
        gp[starts[j] + (i0 - j) * NB:starts[j] + (i1 - j) * NB, :] = lax.dot_general(
            s_ref[:, i0 * NB:i1 * NB], s_ref[:, j * NB:(j + 1) * NB], (((0,), (0,)), ((), ())),
            precision=HI, preferred_element_type=F32)

    def copies(phase, g):
        a, n = GROUPS[g]
        q, m = n // NY, n // NY // NZ
        if phase == 1:
            return [rc(gp.at[at(a + q * lax.rem(y + d, NY), q, 8), :], yrv[g].at[d], ys1.at[g, d], yr1.at[g, d], ydev(d))
                    for d in YD]
        if phase == 2:
            return [rc(ybv[g].at[at(m * lax.rem(z + d, NZ), m, 8), :], zrv[g].at[d], zs1.at[g, d], zr1.at[g, d], zdev(d))
                    for d in ZD]
        if phase == 3:
            here = at(m * z, m, 8)
            return [rc(qfv[g].at[here, :], qfv[g].at[here, :], zs2.at[g, d], zr2.at[g, d], zdev(d)) for d in ZD]
        here = at(a + q * y, q, 8)
        return [rc(qfv[g], gr.at[here, :], ys2.at[g, d], yr2.at[g, d], ydev(d)) for d in YD]

    def send(phase, g):
        for c in copies(phase, g):
            c.start()

    def receive(phase, g):
        for c in copies(phase, g):
            c.wait_recv()

    def phase2(g):
        a, n = GROUPS[g]
        q = n // NY
        receive(1, g)
        ybv[g][...] = gp[at(a + q * y, q, 8), :] + yrv[g][1] + yrv[g][2] + yrv[g][3]
        send(2, g)

    def phase3(g):
        m = GROUPS[g][1] // NY // NZ
        receive(2, g)
        here = at(m * z, m, 8)
        tot = ybv[g][here, :]
        for d in range(1, NZ):
            tot = tot + zrv[g][d]
        qfv[g][here, :] = tot * (1.0 / D)
        send(3, g)

    def phase4(g):
        a, n = GROUPS[g]
        q = n // NY
        receive(3, g)
        send(4, g)
        gr[at(a + q * y, q, 8), :] = qfv[g][...]

    def basis_copy(j, d):
        cols = at(j * NB, NB, NB)
        return rc(bc.at[z, :, cols], bc.at[z, :, cols], bs.at[j, d], br.at[j, d], zdev(d))

    def send_column(j, ref, r0):
        cols = at(j * NB, NB, NB)
        bc[z, :, cols] = ref[r0:r0 + ch, cols].astype(BF16)
        for d in ZD:
            basis_copy(j, d).start()

    sketch_rest(0)
    gram(0, 0, 2)
    send(1, 0)
    send_column(0, s_ref, 0)
    sketch_rest(1)
    gram(0, 2, nb)
    gram(1, 1, nb)
    send(1, 1)
    gram(2, 2, nb)
    send(1, 2)
    gram(3, 3, nb)
    gram(4, 4, nb)
    gp[starts[4] + NB:, :] = jnp.zeros((STACK - starts[4] - NB, NB), F32)
    send(1, 3)
    phase2(0)
    phase2(1)
    for c in f2:
        c.wait_recv()

    def four(i, _):
        o = at(i * 32, 32, 32)
        mw[at(hf * core + qx * x + i * 32, 32, 32), :] = (
            fb[at(qx * x + i * 32, 32, 32), :].astype(F32) + fr[1, o, :].astype(F32) + fr[2, o, :].astype(F32)
            + fr[3, o, :].astype(F32)).astype(BF16)
        return 0
    lax.fori_loop(0, qx // 32, four, 0)
    part = at(hf * core + qx * x, qx, qx)
    f3 = [rc(mw.at[part, :], mw.at[part, :], f3s.at[d], f3r.at[d], xdev(d)) for d in YD]
    for c in f3:
        c.start()
    phase2(2)
    phase3(0)
    phase2(3)
    phase3(1)
    x_ref[0:K, :] = jnp.zeros((K, K), F32)
    x_ref[K:K + ch, :] = s_ref[...]
    l_ref[...] = jnp.zeros((K, K), F32)
    out_ref[...] = jnp.zeros(out_ref.shape, F32)
    phase4(0)
    phase3(2)
    send_column(1, s_ref, 0)
    phase4(1)
    phase3(3)
    send_column(2, s_ref, 0)
    receive(4, 0)
    x_ref[0:2 * NB, 0:NB] = gr[0:2 * NB, :]

    halfrows = at(hf * core, hf, hf)
    f4 = rc(mw.at[halfrows, :], mw.at[halfrows, :], f4s.at[0], f4r.at[0], sib)
    ysrc = z // 2

    def part_copy(j, d):
        cols = at(j * NB, NB, NB)
        return rc(ysb.at[d, :, cols], yrb.at[d, :, cols], ps.at[j, d], pr.at[j, d], ydev(d))

    def orth_copy(j, d):
        cols = at(j * NB, NB, NB)
        t = 4 * lax.rem(z, 2) + lax.rem(y + d, NY)
        return rc(bn.at[at(t * ch, ch, 16), cols], ob.at[:, cols], os_.at[j, d], or_.at[j], ydev(d))

    def factor(j):
        cols = at(j * NB, NB, NB)
        n_ref = ln_ref.at[j]
        t_ref[...] = x_ref[cols, cols]
        base_inverse(t_ref, n_ref)

        @pl.when(j == 0)
        def _():
            phase4(2)
            for c in f3:
                c.wait_recv()
            f4.start()
            f4.wait_recv()

            def delta(i, _):
                o = at(i * step, step, step)
                dz[o, :] = (wv[o, :].astype(F32) - mw[o, :].astype(F32) * (1.0 / (2 * NX))).astype(BF16)
                return 0
            lax.fori_loop(0, rr // step, delta, 0)
            receive(4, 1)
            x_ref[2 * NB:K, 0:NB] = gr[2 * NB:K, :]
        p = lax.dot_general(x_ref[:, cols], n_ref[...], (((1,), (1,)), ((), ())), precision=HI,
                            preferred_element_type=F32)
        r = lax.broadcasted_iota(jnp.int32, (K, NB), 0)
        l_ref[:, cols] = jnp.where(r >= (j + 1) * NB, p[0:K], 0.0)

        for k in range(nb - 1):
            @pl.when(j == k)
            def _(k=k):
                o = (k + 1) * NB
                x_ref[o:, o:] = x_ref[o:, o:] - lax.dot_general(p[o:], p[o:K], (((1,), (1,)), ((), ())), precision=HI,
                                                                preferred_element_type=F32)

        @pl.when(j < nb - AHEAD)
        def _():
            send_column(j + AHEAD, x_ref, K)

    def project(j):
        cols = at(j * NB, NB, NB)
        for d in ZD:
            basis_copy(j, d).wait_recv()
        for t in range(NZ):
            bn[t * NB:(t + 1) * NB, cols] = bc[t, 0:NB, cols]
            bn[NZ * NB + t * ex:NZ * NB + (t + 1) * ex, cols] = bc[t, NB:ch, cols]
        for d in (2, 1, 3):
            ysb[d, :, cols] = jnp.dot(dz[at(lax.rem(y + d, NY) * rows, rows, rows), :], bn[:, cols],
                                      preferred_element_type=F32).astype(BF16)
            part_copy(j, d).start()

        @pl.when(y == ysrc)
        def _():
            for d in YD:
                orth_copy(j, d).start()
            t = 4 * lax.rem(z, 2) + y
            ob[:, cols] = bn[at(t * ch, ch, 16), cols]
        out_ref[ch:, cols] = jnp.dot(dz[mine, :], bn[:, cols], preferred_element_type=F32)

    def finish(j):
        cols = at(j * NB, NB, NB)
        for d in YD:
            part_copy(j, d).wait_recv()

        @pl.when(y != ysrc)
        def _():
            orth_copy(j, 1).wait_recv()
        q = out_ref[ch:, cols] + (yrb[1, :, cols].astype(F32) + yrb[2, :, cols].astype(F32) + yrb[3, :, cols].astype(F32))
        first = jnp.maximum(j - AHEAD + 1, 0) * NB
        seen = at(first, (AHEAD - 1) * NB, NB)
        col = lax.broadcasted_iota(jnp.int32, (NB, (AHEAD - 1) * NB), 1)
        lrow = jnp.where(col + first < j * NB, l_ref[cols, seen], 0.0)
        prior = out_ref[:, seen]
        both = jnp.concatenate([ob[:, cols].astype(F32), q], axis=0) - lax.dot_general(
            prior, lrow, (((1,), (1,)), ((), ())), precision=HI, preferred_element_type=F32)
        out_ref[:, cols] = lax.dot_general(both, ln_ref[j], (((1,), (1,)), ((), ())), precision=HI,
                                           preferred_element_type=F32)

    def column(j, _):
        @pl.when(j == 1)
        def _():
            phase4(3)
            receive(4, 2)
            n = K - NB
            x_ref[NB:K, NB:2 * NB] += gr[starts[1]:starts[1] + n, :]
            x_ref[2 * NB:3 * NB, 2 * NB:3 * NB] += gr[starts[2]:starts[2] + NB, :]
            project(0)

        @pl.when(j == 2)
        def _():
            receive(4, 3)
            x_ref[3 * NB:K, 2 * NB:3 * NB] += gr[starts[2] + NB:starts[3], :]
            x_ref[3 * NB:K, 3 * NB:4 * NB] += gr[starts[3]:starts[4], :]
            x_ref[4 * NB:K, 4 * NB:5 * NB] += gr[starts[4]:starts[4] + NB, :]
            project(1)

        @pl.when(j >= 2)
        def _():
            project(j)
        factor(j)

        @pl.when(j == 1)
        def _():
            finish(0)

        @pl.when(j == 2)
        def _():
            finish(1)

        @pl.when(j >= 2)
        def _():
            finish(j)
        return 0
    lax.fori_loop(0, nb, column, 0)

    done += gcs + gxs + fcs + [c for now in wcs + xs for c in now] + pairs + hs + [f1, f4] + f2 + f3
    for c in done + [c for phase in (1, 2, 3, 4) for g in range(len(GROUPS)) for c in copies(phase, g)]:
        c.wait_send()

    def drain(j, _):
        for d in ZD:
            basis_copy(j, d).wait_send()
        for d in YD:
            part_copy(j, d).wait_send()

        @pl.when(y == ysrc)
        def _():
            for d in YD:
                orth_copy(j, d).wait_send()
        return 0
    lax.fori_loop(0, nb, drain, 0)


def compress(w, g):
    rows, D = w.shape
    K = g.shape[1]
    cw = D // NY
    ch = cw // NZ
    rr = rows * NY
    nb = K // NB
    nu = len(SUBS)
    ng = len(GROUPS)
    V = pl.BlockSpec(memory_space=pltpu.VMEM)
    A = pl.BlockSpec(memory_space=pl.ANY)
    DM = pltpu.SemaphoreType.DMA
    M = pltpu.VMEM
    quarter = [n // NY for _, n in GROUPS]
    return pl.pallas_call(
        body,
        out_shape=jax.ShapeDtypeStruct((ch + rows, K), F32),
        in_specs=[A, A], out_specs=V,
        scratch_shapes=[
            M((rr, cw), BF16), M((rr, K), BF16), M((cw, K), F32), M((2, 4, ch, K), BF16), M((2, 4, ch, K), BF16),
            M((ch, K), F32), M((ch, K), F32), M((80, K), BF16), M((4, 80, K), BF16), M((80, K), F32), M((80, K), F32),
            M((ch, K), F32),
            M((STACK, NB), F32), M((STACK, NB), F32), [M((NY, q, NB), F32) for q in quarter], [M((q, NB), F32) for q in quarter],
            [M((NZ, q // NZ, NB), F32) for q in quarter], [M((q, NB), F32) for q in quarter],
            M((rr // 2, cw), BF16), M((rr // 2, cw), BF16), M((NX, rr // 2 // NX, cw), BF16), M((rr, cw), BF16), M((rr, cw), BF16),
            M((K + ch, K), F32), M((K, K), F32), M((nb, NB, NB), F32), M((NB, NB), F32),
            M((NZ, ch, K), BF16), M((cw, K), BF16), M((NY, rows, K), BF16), M((NY, rows, K), BF16), M((ch, K), BF16),
            DM((9, 4)), DM((9, 4)), DM((4,)), DM((4,)), DM((4, 4)), DM((4, 4)), DM((4,)), DM((4,)),
            DM((2, 4, nu)), DM((2, 4, nu)), DM((nu,)), DM((nu,)), DM((nu, 4)), DM((nu, 4)), DM((nu,)), DM((nu,)),
            DM((10,)), DM((1,)), DM((1,)), DM((4,)), DM((4,)), DM((4,)), DM((4,)), DM((1,)), DM((1,)),
            DM((ng, 4)), DM((ng, 4)), DM((ng, 8)), DM((ng, 8)), DM((ng, 8)), DM((ng, 8)), DM((ng, 4)), DM((ng, 4)),
            DM((nb, 8)), DM((nb, 8)), DM((nb, 4)), DM((nb, 4)), DM((nb, 4)), DM((nb,))],
        compiler_params=pltpu.CompilerParams(collective_id=0, has_side_effects=True, vmem_limit_bytes=60 * 2**20),
        name="delta_compress",
    )(w, g)


def split_body(both_ref, orth_ref, proj_ref):
    ch = orth_ref.shape[0]
    orth_ref[...] = both_ref[:ch, :]
    proj_ref[...] = both_ref[ch:, :]


def split(both, ch):
    n, K = both.shape
    V = pl.BlockSpec(memory_space=pltpu.VMEM)
    return pl.pallas_call(
        split_body,
        out_shape=(jax.ShapeDtypeStruct((ch, K), F32), jax.ShapeDtypeStruct((n - ch, K), F32)),
        in_specs=[V], out_specs=(V, V),
        name="split_outputs",
    )(both)


def on_device(weights, gaussian):
    both = compress(weights[0], gaussian)
    orthonormal, projection = split(both, both.shape[0] - weights.shape[1])
    return (orthonormal[None], projection[None])


def solution(mesh):
    in_specs = (P("expert", "fsdp", None), P("fsdp", None))
    out_specs = (P("expert", "fsdp", None), P("expert", "fsdp", None))
    return jax.shard_map(
        on_device, mesh=mesh, in_specs=in_specs, out_specs=out_specs, check_vma=False
    )
```

```python
import jax
import jax.numpy as jnp
from jax import lax
from jax.sharding import PartitionSpec as P
from jax.experimental import pallas as pl
from jax.experimental.pallas import tpu as pltpu

MESH = pl.DeviceIdType.MESH
NX, NY, NZ = 4, 4, 8
NB = 128
F32, BF16 = jnp.float32, jnp.bfloat16
HI = lax.Precision.HIGHEST
SUBS = ((0, 256), (256, 640))
GROUPS = ((0, 256), (256, 512), (768, 512), (1280, 768))
STACK = 2048
PW = 64
YD = (1, 3, 2)
ZD = (1, 7, 2, 6, 3, 5, 4)


def rc(src, dst, ss, rs, dev):
    return pltpu.make_async_remote_copy(src_ref=src, dst_ref=dst, send_sem=ss, recv_sem=rs, device_id=dev,
                                        device_id_type=MESH)


def at(start, size, unit):
    return pl.ds(pl.multiple_of(start, unit), size)


def wide(v):
    return jnp.broadcast_to(v, (8, NB))


def base_inverse(t_ref, n_ref):
    sub = lax.broadcasted_iota(jnp.int32, (8, NB), 0)
    row = lax.broadcasted_iota(jnp.int32, (NB, NB), 0)
    col = lax.broadcasted_iota(jnp.int32, (NB, NB), 1)
    n_ref[...] = jnp.where(row == col, 1.0, 0.0).astype(F32)
    npan = PW // 8
    for p0 in range(0, NB, PW):
        rt_ = [t_ref[p0 + 8 * s:p0 + 8 * s + 8, :] for s in range(npan)]
        rn_ = [n_ref[p0 + 8 * s:p0 + 8 * s + 8, :] for s in range(npan)]
        c = [wide(rt_[0][:, p0 + i:p0 + i + 1]) for i in range(8)]
        for b in range(npan):
            r0 = p0 + 8 * b
            a = {(k, i): wide(c[i][k:k + 1, :]) for i in range(8) for k in range(i, 8)}
            later = range(b + 1, npan)
            dd = {s: [wide(rt_[s][:, r0 + i:r0 + i + 1]) for i in range(8)] for s in later}
            if b + 1 < npan:
                e = [wide(rt_[b + 1][:, r0 + 8 + i:r0 + 9 + i]) for i in range(8)]
            l = {}
            rs = []
            for i in range(8):
                r = lax.rsqrt(a[i, i])
                rs.append(r)
                for k in range(i + 1, 8):
                    l[k, i] = a[k, i] * r
                for k in range(i + 1, 8):
                    for k2 in range(k, 8):
                        a[k2, k] = a[k2, k] - l[k2, i] * l[k, i]
            rt = [wide(rt_[b][i:i + 1, :]) for i in range(8)]
            rn = [wide(rn_[b][i:i + 1, :]) for i in range(8)]
            for i in range(8):
                rt[i] = rt[i] * rs[i]
                rn[i] = rn[i] * rs[i]
                for k in range(i + 1, 8):
                    rt[k] = rt[k] - l[k, i] * rt[i]
                    rn[k] = rn[k] - l[k, i] * rn[i]
            for s in later:
                d = dd[s]
                for i in range(8):
                    v = d[i] * rs[i]
                    for k in range(i + 1, 8):
                        d[k] = d[k] - v * l[k, i]
                    rt_[s] = rt_[s] - v * rt[i]
                    rn_[s] = rn_[s] - v * rn[i]
                    if s == b + 1:
                        for k in range(8):
                            e[k] = e[k] - v * wide(v[k:k + 1, :])
            ct, cn = rt[0], rn[0]
            for i in range(1, 8):
                ct = jnp.where(sub == i, rt[i], ct)
                cn = jnp.where(sub == i, rn[i], cn)
            rt_[b], rn_[b] = ct, cn
            n_ref[r0:r0 + 8, :] = cn
            if b + 1 < npan:
                c = e
        q0 = p0 + PW
        if q0 < NB:
            lt = jnp.concatenate(rt_, axis=0)
            both = jnp.concatenate([lt, jnp.concatenate(rn_, axis=0)], axis=1)
            upd = lax.dot_general(lt, both, (((0,), (0,)), ((), ())), precision=HI, preferred_element_type=F32)
            t_ref[q0:, :] = t_ref[q0:, :] - upd[q0:, :NB]
            n_ref[q0:, :] = n_ref[q0:, :] - upd[q0:, NB:]


def body(w_ref, g_ref, out_ref,
         wv, gv, p_ref, sbuf, rbuf, sp, sx, tb, tr, mo, mr, s_ref,
         gp, gr, yrv, ybv, zrv, qfv,
         fw, fb, fr, mw, dz, x_ref, l_ref, ln_ref, t_ref, bn, ysb, yrb, ob,
         wsend, wrecv, gsend, grecv, gxsend, gxrecv, fsend, frecv, zsend, zrecv, csend, crecv, xsend, xrecv, hsend, hrecv,
         loc, f1s, f1r, f2s, f2r, f3s, f3r, f4s, f4r, ys1, yr1, zs1, zr1, zs2, zr2, ys2, yr2, bs, br, ps, pr, os_, or_):
    rows, D = w_ref.shape
    K = g_ref.shape[1]
    cw = D // NY
    ch = cw // NZ
    ex = ch - NB
    rr = rows * NY
    nb = K // NB
    e = lax.axis_index("expert")
    f = lax.axis_index("fsdp")
    x, core, y, z = e // 2, lax.rem(e, 2), lax.rem(f, NY), f // NY
    xdev = lambda d: (lax.rem(x + d, NX) * 2 + core, f)
    ydev = lambda d: (e, z * NY + lax.rem(y + d, NY))
    zdev = lambda d: (e, lax.rem(z + d, NZ) * NY + y)
    sib = (e + 1 - 2 * core, f)

    lg = pltpu.make_async_copy(g_ref, gv.at[at(y * rows, rows, rows), :], loc.at[0])
    lg.start()
    barrier = pltpu.get_barrier_semaphore()
    partners = [ydev(d) for d in YD] + [zdev(d) for d in ZD] + [xdev(d) for d in YD] + [sib]
    for p in partners:
        pl.semaphore_signal(barrier, inc=1, device_id=p, device_id_type=MESH)
    pl.semaphore_wait(barrier, len(partners))

    hr, qr = rows // 2, rows // 8
    mine = at(y * rows, rows, rows)
    mypart = core * hr + x * qr
    done = []
    gcs = []
    for d in YD:
        c = rc(g_ref.at[at(mypart, qr, qr), :], gv.at[at(y * rows + mypart, qr, qr), :], gsend.at[d], grecv.at[d], ydev(d))
        c.start()
        gcs.append(c)
    seq = [NZ] + [lax.rem(z + k, NZ) for k in (4, 3, 5, 2, 6, 1, 7, 0)]
    wcs, lws = [], []
    for k, b in enumerate(seq):
        lw = pltpu.make_async_copy(w_ref.at[:, at(y * cw + b * NB, NB, NB)], wv.at[mine, at(b * NB, NB, NB)], loc.at[1 + k])
        lw.start()
        lws.append(lw)
        now = []
        for d in YD:
            yy = lax.rem(y + d, NY)
            c = rc(w_ref.at[:, at(yy * cw + b * NB, NB, NB)], wv.at[mine, at(b * NB, NB, NB)],
                   wsend.at[k, d], wrecv.at[k, d], ydev(d))
            c.start()
            now.append(c)
        wcs.append(now)
    gxs = []
    for i, d in enumerate(YD):
        gcs[i].wait_recv()
        piece = at(lax.rem(y - d + NY, NY) * rows + mypart, qr, qr)
        for dx in YD:
            c = rc(gv.at[piece, :], gv.at[piece, :], gxsend.at[d, dx], gxrecv.at[d, dx], xdev(dx))
            c.start()
            gxs.append(c)
    fcs = []
    for i, d in enumerate(YD):
        for c in gxs[3 * i:3 * i + 3]:
            c.wait_recv()
        piece = at(lax.rem(y - d + NY, NY) * rows + core * hr, hr, hr)
        c = rc(gv.at[piece, :], gv.at[piece, :], fsend.at[d], frecv.at[d], sib)
        c.start()
        fcs.append(c)
    lg.wait()
    for c in fcs:
        c.wait_recv()

    def product(k):
        lws[k].wait()
        for c in wcs[k]:
            c.wait_recv()
        o = at(seq[k] * NB, NB, NB)
        p_ref[o, :] = lax.dot_general(wv[:, o], gv[...], (((0,), (0,)), ((), ())), preferred_element_type=F32)

    ha = 64
    prev = {}

    def own(t, r, n, c0, c1):
        head = p_ref[at(t * NB + r, min(n, NB - r), 16), c0:c1]
        if r + n <= NB:
            return head
        return jnp.concatenate([head, p_ref[at(NZ * NB + t * ex, ex, 16), c0:c1]], axis=0)

    product(0)
    for s in range(4):
        for k in ((1,), (2, 3), (4, 5), (6, 7))[s]:
            product(k)
        for u, (c0, c1) in enumerate(SUBS):
            for dr, d in ((0, 1), (1, NZ - 1)):
                t = lax.rem(z + (4 - s if dr == 0 else NZ - 4 + s), NZ)
                a, m = (0, ha) if dr == 0 else (ha, ch - ha)
                q, l = (ha, ch - ha) if dr == 0 else (0, ha)
                if s:
                    prev[dr, u].wait_recv()
                if s == 0:
                    sbuf[dr, s, a:a + m, c0:c1] = own(t, a, m, c0, c1).astype(BF16)
                    r, n = a, m
                elif s == 1:
                    sbuf[dr, s, a:a + m, c0:c1] = (own(t, a, m, c0, c1) + rbuf[dr, 0, a:a + m, c0:c1].astype(F32)).astype(BF16)
                    sbuf[dr, s, q:q + l, c0:c1] = own(t, q, l, c0, c1).astype(BF16)
                    r, n = 0, ch
                else:
                    sbuf[dr, s, :, c0:c1] = (own(t, 0, ch, c0, c1) + rbuf[dr, s - 1, :, c0:c1].astype(F32)).astype(BF16)
                    r, n = 0, ch
                c = rc(sbuf.at[dr, s, pl.ds(r, n), pl.ds(c0, c1 - c0)], rbuf.at[dr, s, pl.ds(r, n), pl.ds(c0, c1 - c0)],
                       zsend.at[dr, s, u], zrecv.at[dr, s, u], zdev(d))
                c.start()
                done.append(c)
                prev[dr, u] = c
    product(8)
    hf = rr // 2
    f1 = rc(wv.at[at(hf * (1 - core), hf, hf), :], fw, f1s.at[0], f1r.at[0], sib)
    f1.start()
    hm = 80
    half = at((ch - hm) * core, hm, 16)
    rest = at(hm * (1 - core), ch - hm, 16)
    pairs = []
    for u, (c0, c1) in enumerate(SUBS):
        prev[0, u].wait_recv()
        prev[1, u].wait_recv()
        sp[:, c0:c1] = (own(z, 0, ch, c0, c1) + rbuf[0, 3, :, c0:c1].astype(F32) + rbuf[1, 3, :, c0:c1].astype(F32))
        c = rc(sp.at[:, pl.ds(c0, c1 - c0)], sx.at[:, pl.ds(c0, c1 - c0)], csend.at[u], crecv.at[u], sib)
        c.start()
        pairs.append(c)
    xs = []
    for u, (c0, c1) in enumerate(SUBS):
        pairs[u].wait_recv()
        mo[:, c0:c1] = sp[half, c0:c1] + sx[half, c0:c1]
        tb[:, c0:c1] = mo[:, c0:c1].astype(BF16)
        now = []
        for d in YD:
            c = rc(tb.at[:, pl.ds(c0, c1 - c0)], tr.at[d, :, pl.ds(c0, c1 - c0)], xsend.at[u, d], xrecv.at[u, d], xdev(d))
            c.start()
            now.append(c)
        xs.append(now)
    f1.wait_recv()
    step = 64

    def pair(i, _):
        o = at(i * step, step, step)
        fb[o, :] = (wv[at(hf * core + i * step, step, step), :].astype(F32) + fw[o, :].astype(F32)).astype(BF16)
        return 0
    lax.fori_loop(0, hf // step, pair, 0)
    qx = hf // NX
    f2 = [rc(fb.at[at(qx * lax.rem(x + d, NX), qx, qx), :], fr.at[d], f2s.at[d], f2r.at[d], xdev(d)) for d in YD]
    for c in f2:
        c.start()
    hs = []
    for u, (c0, c1) in enumerate(SUBS):
        for c in xs[u]:
            c.wait_recv()
        mo[:, c0:c1] = (mo[:, c0:c1] + tr[1, :, c0:c1].astype(F32) + tr[2, :, c0:c1].astype(F32)
                        + tr[3, :, c0:c1].astype(F32)) * (1.0 / (2 * NX))
        c = rc(mo.at[:, pl.ds(c0, c1 - c0)], mr.at[:, pl.ds(c0, c1 - c0)], hsend.at[u], hrecv.at[u], sib)
        c.start()
        hs.append(c)
        s_ref[half, c0:c1] = sp[half, c0:c1] - mo[:, c0:c1]

    def sketch_rest(u):
        c0, c1 = SUBS[u]
        hs[u].wait_recv()
        s_ref[rest, c0:c1] = sp[rest, c0:c1] - mr[at((2 * hm - ch) * (1 - core), ch - hm, 16), c0:c1]

    starts = [sum(K - i * NB for i in range(j)) for j in range(nb)]

    def gram(j, i0, i1):
        gp[starts[j] + (i0 - j) * NB:starts[j] + (i1 - j) * NB, :] = lax.dot_general(
            s_ref[:, i0 * NB:i1 * NB], s_ref[:, j * NB:(j + 1) * NB], (((0,), (0,)), ((), ())),
            precision=HI, preferred_element_type=F32)

    def copies(phase, g):
        a, n = GROUPS[g]
        q, m = n // NY, n // NY // NZ
        if phase == 1:
            return [rc(gp.at[at(a + q * lax.rem(y + d, NY), q, 8), :], yrv[g].at[d], ys1.at[g, d], yr1.at[g, d], ydev(d))
                    for d in YD]
        if phase == 2:
            return [rc(ybv[g].at[at(m * lax.rem(z + d, NZ), m, 8), :], zrv[g].at[d], zs1.at[g, d], zr1.at[g, d], zdev(d))
                    for d in ZD]
        if phase == 3:
            here = at(m * z, m, 8)
            return [rc(qfv[g].at[here, :], qfv[g].at[here, :], zs2.at[g, d], zr2.at[g, d], zdev(d)) for d in ZD]
        here = at(a + q * y, q, 8)
        return [rc(qfv[g], gr.at[here, :], ys2.at[g, d], yr2.at[g, d], ydev(d)) for d in YD]

    def send(phase, g):
        for c in copies(phase, g):
            c.start()

    def receive(phase, g):
        for c in copies(phase, g):
            c.wait_recv()

    def phase2(g):
        a, n = GROUPS[g]
        q = n // NY
        receive(1, g)
        ybv[g][...] = gp[at(a + q * y, q, 8), :] + yrv[g][1] + yrv[g][2] + yrv[g][3]
        send(2, g)

    def phase3(g):
        m = GROUPS[g][1] // NY // NZ
        receive(2, g)
        here = at(m * z, m, 8)
        tot = ybv[g][here, :]
        for d in range(1, NZ):
            tot = tot + zrv[g][d]
        qfv[g][here, :] = tot * (1.0 / D)
        send(3, g)

    def phase4(g):
        a, n = GROUPS[g]
        q = n // NY
        receive(3, g)
        send(4, g)
        gr[at(a + q * y, q, 8), :] = qfv[g][...]

    def gather_copies(step, dr):
        b = lax.rem(z + (NZ - step if dr == 0 else step), NZ)
        r, n = (0, NB) if step < 3 else ((0, ha) if dr == 0 else (ha, NB - ha))
        pieces = [at(b * NB + r, n, 16)]
        if step < 3 or dr == 1:
            pieces.append(at(NZ * NB + b * ex, ex, 16))
        to = zdev(1 if dr == 0 else NZ - 1)
        return [rc(bn.at[o, :], bn.at[o, :], bs.at[step, dr, i], br.at[step, dr, i], to) for i, o in enumerate(pieces)]

    def gather(step):
        for dr in (0, 1):
            if step:
                for c in gather_copies(step - 1, dr):
                    c.wait_recv()
            for c in gather_copies(step, dr):
                c.start()

    sketch_rest(0)
    gram(0, 0, 2)
    send(1, 0)
    sketch_rest(1)
    bn[at(z * NB, NB, NB), :] = s_ref[0:NB, :].astype(BF16)
    bn[at(NZ * NB + z * ex, ex, 16), :] = s_ref[NB:, :].astype(BF16)
    gather(0)
    gram(0, 2, nb)
    gram(1, 1, nb)
    send(1, 1)
    gram(2, 2, nb)
    send(1, 2)
    gram(3, 3, nb)
    gram(4, 4, nb)
    gp[starts[4] + NB:, :] = jnp.zeros((STACK - starts[4] - NB, NB), F32)
    send(1, 3)
    phase2(0)
    phase2(1)
    gather(1)
    for c in f2:
        c.wait_recv()

    def four(i, _):
        o = at(i * 32, 32, 32)
        mw[at(hf * core + qx * x + i * 32, 32, 32), :] = (
            fb[at(qx * x + i * 32, 32, 32), :].astype(F32) + fr[1, o, :].astype(F32) + fr[2, o, :].astype(F32)
            + fr[3, o, :].astype(F32)).astype(BF16)
        return 0
    lax.fori_loop(0, qx // 32, four, 0)
    part = at(hf * core + qx * x, qx, qx)
    f3 = [rc(mw.at[part, :], mw.at[part, :], f3s.at[d], f3r.at[d], xdev(d)) for d in YD]
    for c in f3:
        c.start()
    phase2(2)
    phase3(0)
    phase2(3)
    phase3(1)
    gather(2)
    x_ref[0:K, :] = jnp.zeros((K, K), F32)
    phase4(0)
    phase3(2)
    phase4(1)
    gather(3)
    phase3(3)
    receive(4, 0)
    x_ref[0:2 * NB, 0:NB] = gr[0:2 * NB, :]

    halfrows = at(hf * core, hf, hf)
    f4 = rc(mw.at[halfrows, :], mw.at[halfrows, :], f4s.at[0], f4r.at[0], sib)
    ysrc = z // 2

    def part_copy(j, d):
        cols = at(j * NB, NB, NB)
        return rc(ysb.at[d, :, cols], yrb.at[d, :, cols], ps.at[j, d], pr.at[j, d], ydev(d))

    def orth_copy(d):
        t = 4 * lax.rem(z, 2) + lax.rem(y + d, NY)
        return rc(bn.at[at(t * ch, ch, 16), :], ob, os_.at[d], or_.at[0], ydev(d))

    def place_rows():
        for dr in (0, 1):
            for c in gather_copies(3, dr):
                c.wait_recv()

        @pl.when(y == ysrc)
        def _():
            for d in YD:
                orth_copy(d).start()
            t = 4 * lax.rem(z, 2) + y
            ob[...] = bn[at(t * ch, ch, 16), :]

    def project():
        for d in (2, 1, 3):
            ysb[d] = jnp.dot(dz[at(lax.rem(y + d, NY) * rows, rows, rows), :], bn[...], preferred_element_type=F32).astype(BF16)
            for j in range(nb):
                part_copy(j, d).start()

        out_ref[ch:, :] = jnp.dot(dz[mine, :], bn[...], preferred_element_type=F32)

    def finish(k):
        cols = slice(k * NB, (k + 1) * NB)
        if k == 0:
            @pl.when(y != ysrc)
            def _():
                orth_copy(1).wait_recv()
            out_ref[:ch, :] = ob[...].astype(F32)
        for d in YD:
            part_copy(k, d).wait_recv()
        out_ref[ch:, cols] += (yrb[1, :, cols].astype(F32) + yrb[2, :, cols].astype(F32) + yrb[3, :, cols].astype(F32))
        out_ref[:, cols] = lax.dot_general(out_ref[:, cols], ln_ref[k], (((1,), (1,)), ((), ())), precision=HI,
                                           preferred_element_type=F32)
        if k < nb - 1:
            after = (k + 1) * NB
            out_ref[:, after:] -= lax.dot_general(out_ref[:, cols], l_ref[after:, cols], (((1,), (1,)), ((), ())),
                                                  precision=HI, preferred_element_type=F32)

    def factor(j):
        cols = at(j * NB, NB, NB)
        n_ref = ln_ref.at[j]
        t_ref[...] = x_ref[cols, cols]
        base_inverse(t_ref, n_ref)

        @pl.when(j == 0)
        def _():
            phase4(2)
            place_rows()
            for c in f3:
                c.wait_recv()
            f4.start()
            f4.wait_recv()

            def delta(i, _):
                o = at(i * step, step, step)
                dz[o, :] = (wv[o, :].astype(F32) - mw[o, :].astype(F32) * (1.0 / (2 * NX))).astype(BF16)
                return 0
            lax.fori_loop(0, rr // step, delta, 0)
            phase4(3)
            receive(4, 1)
            x_ref[2 * NB:K, 0:NB] = gr[2 * NB:K, :]
        for k in range(nb - 1):
            @pl.when(j == k)
            def _(k=k):
                a, b = k * NB, (k + 1) * NB
                p = lax.dot_general(x_ref[b:, a:b], n_ref[...], (((1,), (1,)), ((), ())), precision=HI,
                                    preferred_element_type=F32)
                l_ref[b:, a:b] = p
                x_ref[b:, b:] = x_ref[b:, b:] - lax.dot_general(p, p, (((1,), (1,)), ((), ())), precision=HI,
                                                                preferred_element_type=F32)

    def column(j, _):
        @pl.when(j == 1)
        def _():
            project()
            receive(4, 2)
            n = K - NB
            x_ref[NB:K, NB:2 * NB] += gr[starts[1]:starts[1] + n, :]
            x_ref[2 * NB:3 * NB, 2 * NB:3 * NB] += gr[starts[2]:starts[2] + NB, :]

        @pl.when(j == 2)
        def _():
            receive(4, 3)
            x_ref[3 * NB:K, 2 * NB:3 * NB] += gr[starts[2] + NB:starts[3], :]
            x_ref[3 * NB:K, 3 * NB:4 * NB] += gr[starts[3]:starts[4], :]
            x_ref[4 * NB:K, 4 * NB:5 * NB] += gr[starts[4]:starts[4] + NB, :]

        factor(j)
        for k in range(nb - 2):
            @pl.when(j == k + 2)
            def _(k=k):
                finish(k)
        return 0
    lax.fori_loop(0, nb, column, 0)
    finish(nb - 2)
    finish(nb - 1)

    done += gcs + gxs + fcs + [c for now in wcs + xs for c in now] + pairs + hs + [f1, f4] + f2 + f3
    for c in done + [c for phase in (1, 2, 3, 4) for g in range(len(GROUPS)) for c in copies(phase, g)]:
        c.wait_send()

    for dr in (0, 1):
        for step in range(4):
            for c in gather_copies(step, dr):
                c.wait_send()
    for j in range(nb):
        for d in YD:
            part_copy(j, d).wait_send()

    @pl.when(y == ysrc)
    def _():
        for d in YD:
            orth_copy(d).wait_send()


def compress(w, g):
    rows, D = w.shape
    K = g.shape[1]
    cw = D // NY
    ch = cw // NZ
    rr = rows * NY
    nb = K // NB
    nu = len(SUBS)
    ng = len(GROUPS)
    V = pl.BlockSpec(memory_space=pltpu.VMEM)
    A = pl.BlockSpec(memory_space=pl.ANY)
    DM = pltpu.SemaphoreType.DMA
    M = pltpu.VMEM
    quarter = [n // NY for _, n in GROUPS]
    return pl.pallas_call(
        body,
        out_shape=jax.ShapeDtypeStruct((ch + rows, K), F32),
        in_specs=[A, A], out_specs=V,
        scratch_shapes=[
            M((rr, cw), BF16), M((rr, K), BF16), M((cw, K), F32), M((2, 4, ch, K), BF16), M((2, 4, ch, K), BF16),
            M((ch, K), F32), M((ch, K), F32), M((80, K), BF16), M((4, 80, K), BF16), M((80, K), F32), M((80, K), F32),
            M((ch, K), F32),
            M((STACK, NB), F32), M((STACK, NB), F32), [M((NY, q, NB), F32) for q in quarter], [M((q, NB), F32) for q in quarter],
            [M((NZ, q // NZ, NB), F32) for q in quarter], [M((q, NB), F32) for q in quarter],
            M((rr // 2, cw), BF16), M((rr // 2, cw), BF16), M((NX, rr // 2 // NX, cw), BF16), M((rr, cw), BF16), M((rr, cw), BF16),
            M((K, K), F32), M((K, K), F32), M((nb, NB, NB), F32), M((NB, NB), F32),
            M((cw, K), BF16), M((NY, rows, K), BF16), M((NY, rows, K), BF16), M((ch, K), BF16),
            DM((9, 4)), DM((9, 4)), DM((4,)), DM((4,)), DM((4, 4)), DM((4, 4)), DM((4,)), DM((4,)),
            DM((2, 4, nu)), DM((2, 4, nu)), DM((nu,)), DM((nu,)), DM((nu, 4)), DM((nu, 4)), DM((nu,)), DM((nu,)),
            DM((10,)), DM((1,)), DM((1,)), DM((4,)), DM((4,)), DM((4,)), DM((4,)), DM((1,)), DM((1,)),
            DM((ng, 4)), DM((ng, 4)), DM((ng, 8)), DM((ng, 8)), DM((ng, 8)), DM((ng, 8)), DM((ng, 4)), DM((ng, 4)),
            DM((4, 2, 2)), DM((4, 2, 2)), DM((nb, 4)), DM((nb, 4)), DM((4,)), DM((1,))],
        compiler_params=pltpu.CompilerParams(collective_id=0, has_side_effects=True, vmem_limit_bytes=60 * 2**20),
        name="delta_compress",
    )(w, g)


def split_body(both_ref, orth_ref, proj_ref):
    ch = orth_ref.shape[0]
    orth_ref[...] = both_ref[:ch, :]
    proj_ref[...] = both_ref[ch:, :]


def split(both, ch):
    n, K = both.shape
    V = pl.BlockSpec(memory_space=pltpu.VMEM)
    return pl.pallas_call(
        split_body,
        out_shape=(jax.ShapeDtypeStruct((ch, K), F32), jax.ShapeDtypeStruct((n - ch, K), F32)),
        in_specs=[V], out_specs=(V, V),
        name="split_outputs",
    )(both)


def on_device(weights, gaussian):
    both = compress(weights[0], gaussian)
    orthonormal, projection = split(both, both.shape[0] - weights.shape[1])
    return (orthonormal[None], projection[None])


def solution(mesh):
    in_specs = (P("expert", "fsdp", None), P("fsdp", None))
    out_specs = (P("expert", "fsdp", None), P("expert", "fsdp", None))
    return jax.shard_map(
        on_device, mesh=mesh, in_specs=in_specs, out_specs=out_specs, check_vma=False
    )
```

```python
import jax
import jax.numpy as jnp
from jax import lax
from jax.sharding import PartitionSpec as P
from jax.experimental import pallas as pl
from jax.experimental.pallas import tpu as pltpu

MESH = pl.DeviceIdType.MESH
NX, NY, NZ = 4, 4, 8
NB = 128
F32, BF16 = jnp.float32, jnp.bfloat16
HI = lax.Precision.HIGHEST
SUBS = ((0, 256), (256, 640))
GROUPS = ((0, 256), (256, 512), (768, 512), (1280, 768))
STACK = 2048
PW = 64
YD = (1, 3, 2)
ZD = (1, 7, 2, 6, 3, 5, 4)


def rc(src, dst, ss, rs, dev):
    return pltpu.make_async_remote_copy(src_ref=src, dst_ref=dst, send_sem=ss, recv_sem=rs, device_id=dev,
                                        device_id_type=MESH)


def at(start, size, unit):
    return pl.ds(pl.multiple_of(start, unit), size)


def wide(v):
    return jnp.broadcast_to(v, (8, NB))


def base_inverse(t_ref, n_ref):
    sub = lax.broadcasted_iota(jnp.int32, (8, NB), 0)
    row = lax.broadcasted_iota(jnp.int32, (NB, NB), 0)
    col = lax.broadcasted_iota(jnp.int32, (NB, NB), 1)
    n_ref[...] = jnp.where(row == col, 1.0, 0.0).astype(F32)
    npan = PW // 8
    for p0 in range(0, NB, PW):
        rt_ = [t_ref[p0 + 8 * s:p0 + 8 * s + 8, :] for s in range(npan)]
        rn_ = [n_ref[p0 + 8 * s:p0 + 8 * s + 8, :] for s in range(npan)]
        c = [wide(rt_[0][:, p0 + i:p0 + i + 1]) for i in range(8)]
        for b in range(npan):
            r0 = p0 + 8 * b
            a = {(k, i): wide(c[i][k:k + 1, :]) for i in range(8) for k in range(i, 8)}
            later = range(b + 1, npan)
            dd = {s: [wide(rt_[s][:, r0 + i:r0 + i + 1]) for i in range(8)] for s in later}
            if b + 1 < npan:
                e = [wide(rt_[b + 1][:, r0 + 8 + i:r0 + 9 + i]) for i in range(8)]
            l = {}
            rs = []
            for i in range(8):
                r = lax.rsqrt(a[i, i])
                rs.append(r)
                for k in range(i + 1, 8):
                    l[k, i] = a[k, i] * r
                for k in range(i + 1, 8):
                    for k2 in range(k, 8):
                        a[k2, k] = a[k2, k] - l[k2, i] * l[k, i]
            rt = [wide(rt_[b][i:i + 1, :]) for i in range(8)]
            rn = [wide(rn_[b][i:i + 1, :]) for i in range(8)]
            for i in range(8):
                rt[i] = rt[i] * rs[i]
                rn[i] = rn[i] * rs[i]
                for k in range(i + 1, 8):
                    rt[k] = rt[k] - l[k, i] * rt[i]
                    rn[k] = rn[k] - l[k, i] * rn[i]
            for s in later:
                d = dd[s]
                for i in range(8):
                    v = d[i] * rs[i]
                    for k in range(i + 1, 8):
                        d[k] = d[k] - v * l[k, i]
                    rt_[s] = rt_[s] - v * rt[i]
                    rn_[s] = rn_[s] - v * rn[i]
                    if s == b + 1:
                        for k in range(8):
                            e[k] = e[k] - v * wide(v[k:k + 1, :])
            ct, cn = rt[0], rn[0]
            for i in range(1, 8):
                ct = jnp.where(sub == i, rt[i], ct)
                cn = jnp.where(sub == i, rn[i], cn)
            rt_[b], rn_[b] = ct, cn
            n_ref[r0:r0 + 8, :] = cn
            if b + 1 < npan:
                c = e
        q0 = p0 + PW
        if q0 < NB:
            lt = jnp.concatenate(rt_, axis=0)
            both = jnp.concatenate([lt, jnp.concatenate(rn_, axis=0)], axis=1)
            upd = lax.dot_general(lt, both, (((0,), (0,)), ((), ())), precision=HI, preferred_element_type=F32)
            t_ref[q0:, :] = t_ref[q0:, :] - upd[q0:, :NB]
            n_ref[q0:, :] = n_ref[q0:, :] - upd[q0:, NB:]


def body(w_ref, g_ref, out_ref,
         wv, gv, p_ref, sbuf, rbuf, sp, sx, tb, tr, mo, mr, s_ref,
         gp, gr, yrv, ybv, zrv, qfv,
         fw, fb, fr, mw, dz, x_ref, l_ref, ln_ref, t_ref, bn, ysb, yrb, ob,
         wsend, wrecv, gsend, grecv, gxsend, gxrecv, fsend, frecv, zsend, zrecv, csend, crecv, xsend, xrecv, hsend, hrecv,
         loc, f1s, f1r, f2s, f2r, f3s, f3r, f4s, f4r, ys1, yr1, zs1, zr1, zs2, zr2, ys2, yr2, bs, br, ps, pr, os_, or_):
    rows, D = w_ref.shape
    K = g_ref.shape[1]
    cw = D // NY
    ch = cw // NZ
    ex = ch - NB
    rr = rows * NY
    nb = K // NB
    e = lax.axis_index("expert")
    f = lax.axis_index("fsdp")
    x, core, y, z = e // 2, lax.rem(e, 2), lax.rem(f, NY), f // NY
    xdev = lambda d: (lax.rem(x + d, NX) * 2 + core, f)
    ydev = lambda d: (e, z * NY + lax.rem(y + d, NY))
    zdev = lambda d: (e, lax.rem(z + d, NZ) * NY + y)
    sib = (e + 1 - 2 * core, f)

    lg = pltpu.make_async_copy(g_ref, gv.at[at(y * rows, rows, rows), :], loc.at[0])
    lg.start()
    barrier = pltpu.get_barrier_semaphore()
    partners = [ydev(d) for d in YD] + [zdev(d) for d in ZD] + [xdev(d) for d in YD] + [sib]
    for p in partners:
        pl.semaphore_signal(barrier, inc=1, device_id=p, device_id_type=MESH)
    pl.semaphore_wait(barrier, len(partners))

    hr, qr = rows // 2, rows // 8
    mine = at(y * rows, rows, rows)
    mypart = core * hr + x * qr
    done = []
    gcs = []
    for d in YD:
        c = rc(g_ref.at[at(mypart, qr, qr), :], gv.at[at(y * rows + mypart, qr, qr), :], gsend.at[d], grecv.at[d], ydev(d))
        c.start()
        gcs.append(c)
    seq = [NZ] + [lax.rem(z + k, NZ) for k in (4, 3, 5, 2, 6, 1, 7, 0)]
    wcs, lws = [], []
    for k, b in enumerate(seq):
        lw = pltpu.make_async_copy(w_ref.at[:, at(y * cw + b * NB, NB, NB)], wv.at[mine, at(b * NB, NB, NB)], loc.at[1 + k])
        lw.start()
        lws.append(lw)
        now = []
        for d in YD:
            yy = lax.rem(y + d, NY)
            c = rc(w_ref.at[:, at(yy * cw + b * NB, NB, NB)], wv.at[mine, at(b * NB, NB, NB)],
                   wsend.at[k, d], wrecv.at[k, d], ydev(d))
            c.start()
            now.append(c)
        wcs.append(now)
    gxs = []
    for i, d in enumerate(YD):
        gcs[i].wait_recv()
        piece = at(lax.rem(y - d + NY, NY) * rows + mypart, qr, qr)
        for dx in YD:
            c = rc(gv.at[piece, :], gv.at[piece, :], gxsend.at[d, dx], gxrecv.at[d, dx], xdev(dx))
            c.start()
            gxs.append(c)
    fcs = []
    for i, d in enumerate(YD):
        for c in gxs[3 * i:3 * i + 3]:
            c.wait_recv()
        piece = at(lax.rem(y - d + NY, NY) * rows + core * hr, hr, hr)
        c = rc(gv.at[piece, :], gv.at[piece, :], fsend.at[d], frecv.at[d], sib)
        c.start()
        fcs.append(c)
    lg.wait()
    for c in fcs:
        c.wait_recv()

    def product(k):
        lws[k].wait()
        for c in wcs[k]:
            c.wait_recv()
        o = at(seq[k] * NB, NB, NB)
        p_ref[o, :] = lax.dot_general(wv[:, o], gv[...], (((0,), (0,)), ((), ())), preferred_element_type=F32)

    ha = 64
    prev = {}

    def own(t, r, n, c0, c1):
        head = p_ref[at(t * NB + r, min(n, NB - r), 16), c0:c1]
        if r + n <= NB:
            return head
        return jnp.concatenate([head, p_ref[at(NZ * NB + t * ex, ex, 16), c0:c1]], axis=0)

    product(0)
    for s in range(4):
        for k in ((1,), (2, 3), (4, 5), (6, 7))[s]:
            product(k)
        for u, (c0, c1) in enumerate(SUBS):
            for dr, d in ((0, 1), (1, NZ - 1)):
                t = lax.rem(z + (4 - s if dr == 0 else NZ - 4 + s), NZ)
                a, m = (0, ha) if dr == 0 else (ha, ch - ha)
                q, l = (ha, ch - ha) if dr == 0 else (0, ha)
                if s:
                    prev[dr, u].wait_recv()
                if s == 0:
                    sbuf[dr, s, a:a + m, c0:c1] = own(t, a, m, c0, c1).astype(BF16)
                    r, n = a, m
                elif s == 1:
                    sbuf[dr, s, a:a + m, c0:c1] = (own(t, a, m, c0, c1) + rbuf[dr, 0, a:a + m, c0:c1].astype(F32)).astype(BF16)
                    sbuf[dr, s, q:q + l, c0:c1] = own(t, q, l, c0, c1).astype(BF16)
                    r, n = 0, ch
                else:
                    sbuf[dr, s, :, c0:c1] = (own(t, 0, ch, c0, c1) + rbuf[dr, s - 1, :, c0:c1].astype(F32)).astype(BF16)
                    r, n = 0, ch
                c = rc(sbuf.at[dr, s, pl.ds(r, n), pl.ds(c0, c1 - c0)], rbuf.at[dr, s, pl.ds(r, n), pl.ds(c0, c1 - c0)],
                       zsend.at[dr, s, u], zrecv.at[dr, s, u], zdev(d))
                c.start()
                done.append(c)
                prev[dr, u] = c
    product(8)
    hf = rr // 2
    f1 = rc(wv.at[at(hf * (1 - core), hf, hf), :], fw, f1s.at[0], f1r.at[0], sib)
    f1.start()
    hm = 80
    half = at((ch - hm) * core, hm, 16)
    rest = at(hm * (1 - core), ch - hm, 16)
    pairs = []
    for u, (c0, c1) in enumerate(SUBS):
        prev[0, u].wait_recv()
        prev[1, u].wait_recv()
        sp[:, c0:c1] = (own(z, 0, ch, c0, c1) + rbuf[0, 3, :, c0:c1].astype(F32) + rbuf[1, 3, :, c0:c1].astype(F32))
        c = rc(sp.at[:, pl.ds(c0, c1 - c0)], sx.at[:, pl.ds(c0, c1 - c0)], csend.at[u], crecv.at[u], sib)
        c.start()
        pairs.append(c)
    xs = []
    for u, (c0, c1) in enumerate(SUBS):
        pairs[u].wait_recv()
        mo[:, c0:c1] = sp[half, c0:c1] + sx[half, c0:c1]
        tb[:, c0:c1] = mo[:, c0:c1].astype(BF16)
        now = []
        for d in YD:
            c = rc(tb.at[:, pl.ds(c0, c1 - c0)], tr.at[d, :, pl.ds(c0, c1 - c0)], xsend.at[u, d], xrecv.at[u, d], xdev(d))
            c.start()
            now.append(c)
        xs.append(now)
    f1.wait_recv()
    step = 64

    def pair(i, _):
        o = at(i * step, step, step)
        fb[o, :] = (wv[at(hf * core + i * step, step, step), :].astype(F32) + fw[o, :].astype(F32)).astype(BF16)
        return 0
    lax.fori_loop(0, hf // step, pair, 0)
    qx = hf // NX
    f2 = [rc(fb.at[at(qx * lax.rem(x + d, NX), qx, qx), :], fr.at[d], f2s.at[d], f2r.at[d], xdev(d)) for d in YD]
    for c in f2:
        c.start()
    hs = []
    for u, (c0, c1) in enumerate(SUBS):
        for c in xs[u]:
            c.wait_recv()
        mo[:, c0:c1] = (mo[:, c0:c1] + tr[1, :, c0:c1].astype(F32) + tr[2, :, c0:c1].astype(F32)
                        + tr[3, :, c0:c1].astype(F32)) * (1.0 / (2 * NX))
        c = rc(mo.at[:, pl.ds(c0, c1 - c0)], mr.at[:, pl.ds(c0, c1 - c0)], hsend.at[u], hrecv.at[u], sib)
        c.start()
        hs.append(c)
        s_ref[half, c0:c1] = sp[half, c0:c1] - mo[:, c0:c1]

    def sketch_rest(u):
        c0, c1 = SUBS[u]
        hs[u].wait_recv()
        s_ref[rest, c0:c1] = sp[rest, c0:c1] - mr[at((2 * hm - ch) * (1 - core), ch - hm, 16), c0:c1]

    starts = [sum(K - i * NB for i in range(j)) for j in range(nb)]

    def gram(j, i0, i1):
        gp[starts[j] + (i0 - j) * NB:starts[j] + (i1 - j) * NB, :] = lax.dot_general(
            s_ref[:, i0 * NB:i1 * NB], s_ref[:, j * NB:(j + 1) * NB], (((0,), (0,)), ((), ())),
            precision=HI, preferred_element_type=F32)

    def copies(phase, g):
        a, n = GROUPS[g]
        q, m = n // NY, n // NY // NZ
        if phase == 1:
            return [rc(gp.at[at(a + q * lax.rem(y + d, NY), q, 8), :], yrv[g].at[d], ys1.at[g, d], yr1.at[g, d], ydev(d))
                    for d in YD]
        if phase == 2:
            return [rc(ybv[g].at[at(m * lax.rem(z + d, NZ), m, 8), :], zrv[g].at[d], zs1.at[g, d], zr1.at[g, d], zdev(d))
                    for d in ZD]
        if phase == 3:
            here = at(m * z, m, 8)
            return [rc(qfv[g].at[here, :], qfv[g].at[here, :], zs2.at[g, d], zr2.at[g, d], zdev(d)) for d in ZD]
        here = at(a + q * y, q, 8)
        return [rc(qfv[g], gr.at[here, :], ys2.at[g, d], yr2.at[g, d], ydev(d)) for d in YD]

    def send(phase, g):
        for c in copies(phase, g):
            c.start()

    def receive(phase, g):
        for c in copies(phase, g):
            c.wait_recv()

    def phase2(g):
        a, n = GROUPS[g]
        q = n // NY
        receive(1, g)
        ybv[g][...] = gp[at(a + q * y, q, 8), :] + yrv[g][1] + yrv[g][2] + yrv[g][3]
        send(2, g)

    def phase3(g):
        m = GROUPS[g][1] // NY // NZ
        receive(2, g)
        here = at(m * z, m, 8)
        tot = ybv[g][here, :]
        for d in range(1, NZ):
            tot = tot + zrv[g][d]
        qfv[g][here, :] = tot * (1.0 / D)
        send(3, g)

    def phase4(g):
        a, n = GROUPS[g]
        q = n // NY
        receive(3, g)
        send(4, g)
        gr[at(a + q * y, q, 8), :] = qfv[g][...]

    def gather_copies(step, dr):
        b = lax.rem(z + (NZ - step if dr == 0 else step), NZ)
        r, n = (0, NB) if step < 3 else ((0, ha) if dr == 0 else (ha, NB - ha))
        pieces = [at(b * NB + r, n, 16)]
        if step < 3 or dr == 1:
            pieces.append(at(NZ * NB + b * ex, ex, 16))
        to = zdev(1 if dr == 0 else NZ - 1)
        return [rc(bn.at[o, :], bn.at[o, :], bs.at[step, dr, i], br.at[step, dr, i], to) for i, o in enumerate(pieces)]

    def gather(step):
        for dr in (0, 1):
            if step:
                for c in gather_copies(step - 1, dr):
                    c.wait_recv()
            for c in gather_copies(step, dr):
                c.start()

    sketch_rest(0)
    gram(0, 0, 2)
    send(1, 0)
    sketch_rest(1)
    bn[at(z * NB, NB, NB), :] = s_ref[0:NB, :].astype(BF16)
    bn[at(NZ * NB + z * ex, ex, 16), :] = s_ref[NB:, :].astype(BF16)
    gather(0)
    gram(0, 2, nb)
    gram(1, 1, nb)
    send(1, 1)
    gram(2, 2, nb)
    send(1, 2)
    gram(3, 3, nb)
    gram(4, 4, nb)
    gp[starts[4] + NB:, :] = jnp.zeros((STACK - starts[4] - NB, NB), F32)
    send(1, 3)
    phase2(0)
    phase2(1)
    gather(1)
    phase2(2)
    phase3(0)
    for c in f2:
        c.wait_recv()

    def four(i, _):
        o = at(i * 32, 32, 32)
        mw[at(hf * core + qx * x + i * 32, 32, 32), :] = (
            fb[at(qx * x + i * 32, 32, 32), :].astype(F32) + fr[1, o, :].astype(F32) + fr[2, o, :].astype(F32)
            + fr[3, o, :].astype(F32)).astype(BF16)
        return 0
    lax.fori_loop(0, qx // 32, four, 0)
    part = at(hf * core + qx * x, qx, qx)
    f3 = [rc(mw.at[part, :], mw.at[part, :], f3s.at[d], f3r.at[d], xdev(d)) for d in YD]
    for c in f3:
        c.start()
    phase2(3)
    phase3(1)
    gather(2)
    x_ref[0:K, :] = jnp.zeros((K, K), F32)
    phase4(0)
    phase3(2)
    phase4(1)
    gather(3)
    phase3(3)
    receive(4, 0)
    x_ref[0:2 * NB, 0:NB] = gr[0:2 * NB, :]

    halfrows = at(hf * core, hf, hf)
    f4 = rc(mw.at[halfrows, :], mw.at[halfrows, :], f4s.at[0], f4r.at[0], sib)
    ysrc = z // 2

    def part_copy(j, d):
        cols = at(j * NB, NB, NB)
        return rc(ysb.at[d, :, cols], yrb.at[d, :, cols], ps.at[j, d], pr.at[j, d], ydev(d))

    def orth_copy(d):
        t = 4 * lax.rem(z, 2) + lax.rem(y + d, NY)
        return rc(bn.at[at(t * ch, ch, 16), :], ob, os_.at[d], or_.at[0], ydev(d))

    def place_rows():
        for dr in (0, 1):
            for c in gather_copies(3, dr):
                c.wait_recv()

        @pl.when(y == ysrc)
        def _():
            for d in YD:
                orth_copy(d).start()
            t = 4 * lax.rem(z, 2) + y
            ob[...] = bn[at(t * ch, ch, 16), :]

    def project():
        for d in (2, 1, 3):
            ysb[d] = jnp.dot(dz[at(lax.rem(y + d, NY) * rows, rows, rows), :], bn[...], preferred_element_type=F32).astype(BF16)
            for j in range(nb):
                part_copy(j, d).start()

        out_ref[ch:, :] = jnp.dot(dz[mine, :], bn[...], preferred_element_type=F32)

    def finish(k):
        cols = slice(k * NB, (k + 1) * NB)
        if k == 0:
            @pl.when(y != ysrc)
            def _():
                orth_copy(1).wait_recv()
            out_ref[:ch, :] = ob[...].astype(F32)
        for d in YD:
            part_copy(k, d).wait_recv()
        out_ref[ch:, cols] += (yrb[1, :, cols].astype(F32) + yrb[2, :, cols].astype(F32) + yrb[3, :, cols].astype(F32))
        out_ref[:, cols] = lax.dot_general(out_ref[:, cols], ln_ref[k], (((1,), (1,)), ((), ())), precision=HI,
                                           preferred_element_type=F32)
        if k < nb - 1:
            after = (k + 1) * NB
            out_ref[:, after:] -= lax.dot_general(out_ref[:, cols], l_ref[after:, cols], (((1,), (1,)), ((), ())),
                                                  precision=HI, preferred_element_type=F32)

    def factor(j):
        cols = at(j * NB, NB, NB)
        n_ref = ln_ref.at[j]
        t_ref[...] = x_ref[cols, cols]
        base_inverse(t_ref, n_ref)

        @pl.when(j == 0)
        def _():
            phase4(2)
            place_rows()
            for c in f3:
                c.wait_recv()
            f4.start()
            f4.wait_recv()

            def delta(i, _):
                o = at(i * step, step, step)
                dz[o, :] = (wv[o, :].astype(F32) - mw[o, :].astype(F32) * (1.0 / (2 * NX))).astype(BF16)
                return 0
            lax.fori_loop(0, rr // step, delta, 0)
            phase4(3)
            receive(4, 1)
            x_ref[2 * NB:K, 0:NB] = gr[2 * NB:K, :]
        for k in range(nb - 1):
            @pl.when(j == k)
            def _(k=k):
                a, b = k * NB, (k + 1) * NB
                p = lax.dot_general(x_ref[b:, a:b], n_ref[...], (((1,), (1,)), ((), ())), precision=HI,
                                    preferred_element_type=F32)
                l_ref[b:, a:b] = p
                x_ref[b:, b:] = x_ref[b:, b:] - lax.dot_general(p, p, (((1,), (1,)), ((), ())), precision=HI,
                                                                preferred_element_type=F32)

    def column(j, _):
        @pl.when(j == 1)
        def _():
            project()
            receive(4, 2)
            n = K - NB
            x_ref[NB:K, NB:2 * NB] += gr[starts[1]:starts[1] + n, :]
            x_ref[2 * NB:3 * NB, 2 * NB:3 * NB] += gr[starts[2]:starts[2] + NB, :]

        @pl.when(j == 2)
        def _():
            receive(4, 3)
            x_ref[3 * NB:K, 2 * NB:3 * NB] += gr[starts[2] + NB:starts[3], :]
            x_ref[3 * NB:K, 3 * NB:4 * NB] += gr[starts[3]:starts[4], :]
            x_ref[4 * NB:K, 4 * NB:5 * NB] += gr[starts[4]:starts[4] + NB, :]

        factor(j)
        for k in range(nb - 2):
            @pl.when(j == k + 2)
            def _(k=k):
                finish(k)
        return 0
    lax.fori_loop(0, nb, column, 0)
    finish(nb - 2)
    finish(nb - 1)

    done += gcs + gxs + fcs + [c for now in wcs + xs for c in now] + pairs + hs + [f1, f4] + f2 + f3
    for c in done + [c for phase in (1, 2, 3, 4) for g in range(len(GROUPS)) for c in copies(phase, g)]:
        c.wait_send()

    for dr in (0, 1):
        for step in range(4):
            for c in gather_copies(step, dr):
                c.wait_send()
    for j in range(nb):
        for d in YD:
            part_copy(j, d).wait_send()

    @pl.when(y == ysrc)
    def _():
        for d in YD:
            orth_copy(d).wait_send()


def compress(w, g):
    rows, D = w.shape
    K = g.shape[1]
    cw = D // NY
    ch = cw // NZ
    rr = rows * NY
    nb = K // NB
    nu = len(SUBS)
    ng = len(GROUPS)
    V = pl.BlockSpec(memory_space=pltpu.VMEM)
    A = pl.BlockSpec(memory_space=pl.ANY)
    DM = pltpu.SemaphoreType.DMA
    M = pltpu.VMEM
    quarter = [n // NY for _, n in GROUPS]
    return pl.pallas_call(
        body,
        out_shape=jax.ShapeDtypeStruct((ch + rows, K), F32),
        in_specs=[A, A], out_specs=V,
        scratch_shapes=[
            M((rr, cw), BF16), M((rr, K), BF16), M((cw, K), F32), M((2, 4, ch, K), BF16), M((2, 4, ch, K), BF16),
            M((ch, K), F32), M((ch, K), F32), M((80, K), BF16), M((4, 80, K), BF16), M((80, K), F32), M((80, K), F32),
            M((ch, K), F32),
            M((STACK, NB), F32), M((STACK, NB), F32), [M((NY, q, NB), F32) for q in quarter], [M((q, NB), F32) for q in quarter],
            [M((NZ, q // NZ, NB), F32) for q in quarter], [M((q, NB), F32) for q in quarter],
            M((rr // 2, cw), BF16), M((rr // 2, cw), BF16), M((NX, rr // 2 // NX, cw), BF16), M((rr, cw), BF16), M((rr, cw), BF16),
            M((K, K), F32), M((K, K), F32), M((nb, NB, NB), F32), M((NB, NB), F32),
            M((cw, K), BF16), M((NY, rows, K), BF16), M((NY, rows, K), BF16), M((ch, K), BF16),
            DM((9, 4)), DM((9, 4)), DM((4,)), DM((4,)), DM((4, 4)), DM((4, 4)), DM((4,)), DM((4,)),
            DM((2, 4, nu)), DM((2, 4, nu)), DM((nu,)), DM((nu,)), DM((nu, 4)), DM((nu, 4)), DM((nu,)), DM((nu,)),
            DM((10,)), DM((1,)), DM((1,)), DM((4,)), DM((4,)), DM((4,)), DM((4,)), DM((1,)), DM((1,)),
            DM((ng, 4)), DM((ng, 4)), DM((ng, 8)), DM((ng, 8)), DM((ng, 8)), DM((ng, 8)), DM((ng, 4)), DM((ng, 4)),
            DM((4, 2, 2)), DM((4, 2, 2)), DM((nb, 4)), DM((nb, 4)), DM((4,)), DM((1,))],
        compiler_params=pltpu.CompilerParams(collective_id=0, has_side_effects=True, vmem_limit_bytes=60 * 2**20),
        name="delta_compress",
    )(w, g)


def split_body(both_ref, orth_ref, proj_ref):
    ch = orth_ref.shape[0]
    orth_ref[...] = both_ref[:ch, :]
    proj_ref[...] = both_ref[ch:, :]


def split(both, ch):
    n, K = both.shape
    V = pl.BlockSpec(memory_space=pltpu.VMEM)
    return pl.pallas_call(
        split_body,
        out_shape=(jax.ShapeDtypeStruct((ch, K), F32), jax.ShapeDtypeStruct((n - ch, K), F32)),
        in_specs=[V], out_specs=(V, V),
        name="split_outputs",
    )(both)


def on_device(weights, gaussian):
    both = compress(weights[0], gaussian)
    orthonormal, projection = split(both, both.shape[0] - weights.shape[1])
    return (orthonormal[None], projection[None])


def solution(mesh):
    in_specs = (P("expert", "fsdp", None), P("fsdp", None))
    out_specs = (P("expert", "fsdp", None), P("expert", "fsdp", None))
    return jax.shard_map(
        on_device, mesh=mesh, in_specs=in_specs, out_specs=out_specs, check_vma=False
    )
```
